128 devices in a mesh: seq: 16 (over z, x_lo, core), head: 4 (over y), cfg: 2 (over x_hi).
Axes of the slice: x: 4 (x_hi: 2, x_lo: 2; x = x_hi * 2 + x_lo), y: 4, z: 4, core: 2. Of those that a mesh axis runs over, the one named last changes fastest.
Arguments:
- query: bfloat16 [2, 4096, 1536], P('cfg', 'seq', 'head')
- key: bfloat16 [2, 4096, 1536], P('cfg', 'seq', 'head')
- value: bfloat16 [2, 4096, 1536], P('cfg', 'seq', 'head'), may hold values from -6 to 6
- cotangent: bfloat16 [4096, 3072], P('seq', ('head', 'cfg')), may hold values from -6 to 6
- key_block_slots: int32 [32, 16], P('seq'), may hold values from 0 to 31, as said below
- live_key_counts: int32 [32], P('seq'), may hold values from 1 to 16, as said below
- guidance_index: int32 [1], replicated, may hold values from 0 to 12
- output_weight_rows: bfloat16 [1536, 3072], P('head'), may hold values from -0.15625 to 0.15625
- lowering_matrix: bfloat16 [1536, 64], P('head'), may hold values from -0.15625 to 0.15625
- raising_matrix: bfloat16 [64, 3072], replicated, may hold values from -0.75 to 0.75
Outputs:
- grad_query: bfloat16 [2, 4096, 1536], P('cfg', 'seq', 'head')
- grad_key: bfloat16 [2, 4096, 1536], P('cfg', 'seq', 'head')
- grad_value: bfloat16 [2, 4096, 1536], P('cfg', 'seq', 'head')
- lowering_matrix_slope: float32 [1536, 64], P('head')
- grad_up: float32 [64, 3072], replicated
The draws below stay inside these ranges and needn't reach their ends.
Inputs may be any that keep to these rules, and one draw needn't show every extreme that they name: `key_block_slots`: row i lists 16 different key blocks; slot 0 is block i itself. `live_key_counts`: query blocks of one index of seq share a density drawn for that index; some query block uses all 16 slots.
All inputs are finite; a program needn't handle non-finite values.
Results may differ from the reference program's by a relative error of at most 0.025.
Values may be sent and summed in bfloat16 or wider, within the bound.
A program may use at most 128 MiB of HBM per device.

```python
import jax
import jax.numpy as jnp
from jax import lax

MODEL_WIDTH = 3072
HEAD_COUNT = 12
HEAD_SIZE = 128
ADAPTER_RANK = 64
BLK = 128
MAXK = 16
QB_DEV = 2
TOKENS = 4096
QB = 32


def shared_keys(key):
    return jax.random.normal(key, (2, TOKENS, HEAD_COUNT * HEAD_SIZE), jnp.float32)


def draw_key(key, part):
    base = shared_keys(key)
    return base.astype(jnp.bfloat16)


def draw_query(key, part):
    key = jax.random.fold_in(key, 11)
    second = jax.random.fold_in(key, 1)
    fresh = jax.random.normal(second, (2, TOKENS, HEAD_COUNT * HEAD_SIZE), jnp.float32)
    return fresh.astype(jnp.bfloat16)


def draw_key_block_slots(key, part):
    key = jax.random.fold_in(key, 23)
    raw = jax.random.randint(key, (QB, QB - 1), 0, 4096)
    made = raw * QB + jnp.arange(QB - 1)[None, :]
    order = jnp.argsort(made, axis=1).astype(jnp.int32)
    offsets = jnp.concatenate([jnp.zeros((QB, 1), jnp.int32), order + 1], axis=1)[:, :MAXK]
    return ((jnp.arange(QB, dtype=jnp.int32)[:, None] + offsets) % QB).astype(jnp.int32)


def draw_live_key_counts(key, part):
    key = jax.random.fold_in(key, 37)
    first, second, third = jax.random.split(key, 3)
    shards = QB // QB_DEV
    level = jax.random.randint(first, (shards, 1), 1, MAXK + 1)
    raw = jax.random.randint(second, (shards, QB_DEV), 0, 1 << 20)
    counts = (raw % level + 1).reshape(QB)
    where = jax.random.randint(third, (), 0, QB)
    counts = jnp.where(jnp.arange(QB) == where, MAXK, counts)
    return counts.astype(jnp.int32)


def levels(stream_key, extent, cuts, smallest, high):
    def one(dim, parts):
        steps = jax.random.uniform(jax.random.fold_in(jax.random.fold_in(stream_key, 6), dim), (parts,), jnp.float32, smallest / len(cuts), high / len(cuts))
        return jnp.repeat(jnp.exp(steps), extent[dim] // parts).reshape((-1,) + (1,) * (len(extent) - dim - 1))

    factor_of = one(*cuts[0])
    for cut in cuts[1:]:
        factor_of = factor_of * one(*cut)
    return factor_of


def gaussian(stream_key, dims, spread, limit, cuts=(), kind=jnp.bfloat16):
    drawn = spread * jax.random.normal(stream_key, dims, jnp.float32)
    if cuts:
        drawn = drawn * levels(stream_key, dims, cuts, -0.22, 0.18)
    return jnp.clip(drawn, -limit, limit).astype(kind)


def setup_inputs(seed: int = 0) -> dict:
    key_list = jax.random.split(jax.random.key(seed), 11)
    return {
        "query": draw_query(jax.random.fold_in(key_list[10], 71), 0),
        "key": draw_key(jax.random.fold_in(key_list[10], 71), 0),
        "value": gaussian(key_list[2], (2, TOKENS, HEAD_COUNT * HEAD_SIZE), 1.0, 6.0, ((0, 2), (1, 16), (2, 4))),
        "cotangent": gaussian(key_list[3], (TOKENS, MODEL_WIDTH), 1.0, 6.0, ((0, 16), (1, 8))),
        "key_block_slots": draw_key_block_slots(jax.random.fold_in(key_list[10], 71), 0),
        "live_key_counts": draw_live_key_counts(jax.random.fold_in(key_list[10], 71), 0),
        "guidance_index": jax.random.randint(key_list[6], (1,), 0, 13).astype(jnp.int32),
        "output_weight_rows": gaussian(key_list[7], (HEAD_COUNT * HEAD_SIZE, MODEL_WIDTH), (HEAD_COUNT * HEAD_SIZE) ** -0.5, 0.15625, ((0, 4),)),
        "lowering_matrix": gaussian(key_list[8], (HEAD_COUNT * HEAD_SIZE, ADAPTER_RANK), (HEAD_COUNT * HEAD_SIZE) ** -0.5, 0.15625, ((0, 4),)),
        "raising_matrix": gaussian(key_list[9], (ADAPTER_RANK, MODEL_WIDTH), ADAPTER_RANK ** -0.5, 0.75),
    }


def single_branch(query_tensor, key_tensor, value_tensor, final_cotangent_vector, key_block_slots, live_key_counts, output_weight_rows, lowering_matrix, raising_matrix):
    thirty_two_bit_real = jnp.float32
    truncated_sixteen_bit = jnp.bfloat16
    nblocks = TOKENS // BLK
    scale = HEAD_SIZE ** -0.5
    slots = jnp.arange(MAXK, dtype=jnp.int32)
    q_tiles = query_tensor.reshape(nblocks, BLK, HEAD_COUNT, HEAD_SIZE)
    k_tiles = key_tensor.reshape(nblocks, BLK, HEAD_COUNT, HEAD_SIZE)
    v_tiles = value_tensor.reshape(nblocks, BLK, HEAD_COUNT, HEAD_SIZE)

    def scores(i):
        ids = key_block_slots[i]
        live = slots < live_key_counts[i]
        s = jnp.einsum('qhd,jkhd->hqjk', q_tiles[i].astype(thirty_two_bit_real), k_tiles[ids].astype(thirty_two_bit_real)) * scale
        s = jnp.where(live[None, None, :, None], s, -jnp.inf)
        return s, ids

    def forward(i):
        s, ids = scores(i)
        top = jnp.max(s, axis=(2, 3), keepdims=True)
        lse = top + jnp.log(jnp.sum(jnp.exp(s - top), axis=(2, 3), keepdims=True))
        probs = jnp.exp(s - lse).astype(truncated_sixteen_bit)
        out = jnp.einsum('hqjk,jkhd->qhd', probs.astype(thirty_two_bit_real), v_tiles[ids].astype(thirty_two_bit_real)).astype(truncated_sixteen_bit)
        return out, lse[:, :, 0, 0]

    o_tiles, lse = lax.map(forward, jnp.arange(nblocks, dtype=jnp.int32))
    merged_product_matrix = o_tiles.reshape(TOKENS, HEAD_COUNT * HEAD_SIZE)
    adapter_hidden = jnp.dot(merged_product_matrix, lowering_matrix, preferred_element_type=thirty_two_bit_real).astype(truncated_sixteen_bit)
    narrow_inner_slope = jnp.dot(final_cotangent_vector, raising_matrix.T, preferred_element_type=thirty_two_bit_real).astype(truncated_sixteen_bit)
    d_o = (jnp.dot(final_cotangent_vector, output_weight_rows.T, preferred_element_type=thirty_two_bit_real)
           + jnp.dot(narrow_inner_slope, lowering_matrix.T, preferred_element_type=thirty_two_bit_real)).astype(truncated_sixteen_bit)
    lowering_matrix_slope = jnp.dot(merged_product_matrix.T, narrow_inner_slope, preferred_element_type=thirty_two_bit_real)
    grad_up = jnp.dot(adapter_hidden.T, final_cotangent_vector, preferred_element_type=thirty_two_bit_real)
    do_tiles = d_o.reshape(nblocks, BLK, HEAD_COUNT, HEAD_SIZE)
    delta = jnp.sum(do_tiles.astype(thirty_two_bit_real) * o_tiles.astype(thirty_two_bit_real), axis=3)

    def backward(carry, i):
        dk_acc, dv_acc = carry
        s, ids = scores(i)
        probs = jnp.exp(s - lse[i][:, :, None, None])
        pb = lax.optimization_barrier(probs.astype(truncated_sixteen_bit)).astype(thirty_two_bit_real)
        dob = do_tiles[i].astype(thirty_two_bit_real)
        dp = jnp.einsum('qhd,jkhd->hqjk', dob, v_tiles[ids].astype(thirty_two_bit_real))
        ds = (probs * (dp - jnp.transpose(delta[i])[:, :, None, None])).astype(truncated_sixteen_bit)
        ds = lax.optimization_barrier(ds).astype(thirty_two_bit_real)
        dq = (jnp.einsum('hqjk,jkhd->qhd', ds, k_tiles[ids].astype(thirty_two_bit_real)) * scale).astype(truncated_sixteen_bit)
        dk_acc = dk_acc.at[ids].add(jnp.einsum('hqjk,qhd->jkhd', ds, q_tiles[i].astype(thirty_two_bit_real)) * scale)
        dv_acc = dv_acc.at[ids].add(jnp.einsum('hqjk,qhd->jkhd', pb, dob))
        return (dk_acc, dv_acc), dq

    zeros = jnp.zeros((nblocks, BLK, HEAD_COUNT, HEAD_SIZE), thirty_two_bit_real)
    (dk_acc, dv_acc), dq = lax.scan(backward, (zeros, zeros), jnp.arange(nblocks, dtype=jnp.int32))
    width = HEAD_COUNT * HEAD_SIZE
    return (dq.reshape(TOKENS, width), dk_acc.astype(truncated_sixteen_bit).reshape(TOKENS, width),
            dv_acc.astype(truncated_sixteen_bit).reshape(TOKENS, width), lowering_matrix_slope, grad_up)


def reference(query, key, value, cotangent, key_block_slots, live_key_counts, guidance_index, output_weight_rows, lowering_matrix, raising_matrix):
    weight = 1.5 + 0.5 * guidance_index[0].astype(jnp.float32)
    results = []
    for branch in range(2):
        coef = weight if branch == 0 else 1.0 - weight
        final_cotangent_vector = (coef * cotangent.astype(jnp.float32)).astype(jnp.bfloat16)
        results.append(single_branch(query[branch], key[branch], value[branch], final_cotangent_vector, key_block_slots, live_key_counts,
                                  output_weight_rows, lowering_matrix, raising_matrix))
    first, second = results
    return (jnp.stack([first[0], second[0]]), jnp.stack([first[1], second[1]]),
            jnp.stack([first[2], second[2]]), first[3] + second[3], first[4] + second[4])
```

```python
import functools
import math

import jax
import jax.numpy as jnp
from jax import lax
from jax.experimental import pallas as pl
from jax.experimental.pallas import tpu as pltpu
from jax.sharding import PartitionSpec as P

HD = 128
NH = 3
W = 384
T = 256
NK = 1024
RANK = 64
SCALE = HD ** -0.5
C2 = SCALE * math.log2(math.e)
BIG = 3.0e38
F32 = jnp.float32
BF16 = jnp.bfloat16
MESH = pl.DeviceIdType.MESH
NSEM = 96


def nn(a, b):
    return lax.dot_general(a, b, (((1,), (0,)), ((), ())), preferred_element_type=F32)


def nt(a, b):
    return lax.dot_general(a, b, (((1,), (1,)), ((), ())), preferred_element_type=F32)


def kernel(
    q_in, k_in, v_in, cot_in, w_in, low_in, up_in, slots_ref, counts_ref, guide_ref,
    dq_out, dk_out, dv_out, slope_out, gup_out,
    Q, K, V, KT, VT, COT, WB, LOW, PART, PARTR, DOT, BIAS, PR, OT, STO, STR,
    DK, DV, DQB, DQR, DKB, DVB, DKR, DVR, DKX, DVX, DKXR, DVXR,
    LHB, LHR, LHY, LHYR, LHC, LHCR, GSB, GSR, S1B, S1R, S2B, S2R, GU, SL, SLT,
    send_sem, recv_sem, loc_sem,
):
    s, hy, c = lax.axis_index("seq"), lax.axis_index("head"), lax.axis_index("cfg")
    z, x, kc = s // 4, (s // 2) % 2, s % 2
    g = s % 4
    peer = {}
    for d in (1, 2, 3):
        peer["z%d" % d] = {"seq": ((z + d) % 4) * 4 + g}
        peer["y%d" % d] = {"head": (hy + d) % 4}
    peer["sib"] = {"seq": z * 4 + x * 2 + (1 - kc)}
    peer["x"] = {"seq": z * 4 + (1 - x) * 2 + kc}
    peer["xo"] = {"seq": z * 4 + (1 - x) * 2 + (1 - kc)}
    peer["cfg"] = {"cfg": 1 - c}

    count = [0, 0]
    started = []

    def local(src, dst):
        cp = pltpu.make_async_copy(src, dst, loc_sem.at[count[1]])
        count[1] += 1
        cp.start()
        return cp

    def send(src, dst, to):
        i = count[0]
        count[0] += 1
        cp = pltpu.make_async_remote_copy(
            src_ref=src, dst_ref=dst, send_sem=send_sem.at[i], recv_sem=recv_sem.at[i],
            device_id=peer[to], device_id_type=MESH,
        )
        cp.start()
        started.append(cp)
        return cp

    def ring(axis, src, dst):
        got = {}
        for d in (1, 3, 2):
            e = (4 - d) % 4
            got[e] = send(src(d), dst(e), "%s%d" % (axis, d))
        return got

    l_cot = local(cot_in, COT.at[0])
    l_w = []
    for j in range(4):
        col = pl.multiple_of((((hy + j) % 4) * 2 + c) * W, 128)
        l_w.append(local(w_in.at[:, pl.ds(col, W)], WB.at[j, pl.ds(0, W)]))
        l_w.append(local(up_in.at[:, pl.ds(col, W)], WB.at[j, pl.ds(W, RANK)]))
    l_kv = [local(k_in, K.at[pl.ds(0, T)]), local(v_in, V.at[pl.ds(0, T)])]
    l_q = local(q_in, Q.at[pl.ds(0, T)])
    l_low = local(low_in, LOW)

    barrier = pltpu.get_barrier_semaphore()
    for name in peer:
        pl.semaphore_signal(barrier, inc=1, device_id=peer[name], device_id_type=MESH)
    pl.semaphore_wait(barrier, len(peer))

    r_cot = ring("y", lambda d: cot_in, lambda e: COT.at[e])
    r_k = {}
    r_v = {}
    for to, r in (("x", 2), ("sib", 1)):
        r_k[r] = send(k_in, K.at[pl.ds(r * T, T)], to)
        r_v[r] = send(v_in, V.at[pl.ds(r * T, T)], to)
    r_q = ring("z", lambda d: q_in, lambda e: Q.at[pl.ds(e * T, T)])

    row = lax.broadcasted_iota(jnp.int32, (8, T), 0)
    lane = lax.broadcasted_iota(jnp.int32, (8, T), 1)
    rx, rk = row // 4, (row // 2) % 2
    gx = x + rx - 2 * x * rx
    gk = kc + rk - 2 * kc * rk
    base_block = 2 * (gx * 2 + gk) + row % 2
    for d in range(4):
        block = base_block + 8 * ((z + d) % 4)
        live = jnp.zeros((8, T), F32)
        for qb in range(2):
            n = counts_ref[qb]
            for j in range(16):
                want = jnp.where(j < n, slots_ref[qb, j], -1)
                hit = jnp.logical_and(block == want, lane // 128 == qb)
                live = jnp.where(hit, 1.0, live)
        BIAS[d] = jnp.where(live > 0, BIG, -BIG)
    r_bias = ring("z", lambda d: BIAS.at[d], lambda e: BIAS.at[4 + e])

    weight = 1.5 + 0.5 * guide_ref[0].astype(F32)
    coef = jnp.where(c == 0, weight, 1.0 - weight)

    l_cot.wait()
    for cp in l_w:
        cp.wait()
    acc = nt(WB[0], COT[0])
    for e in (1, 3, 2):
        r_cot[e].wait_recv()
        acc += nt(WB[e], COT[e])
    PART[...] = acc.astype(BF16)
    r_part = send(PART, PARTR, "cfg")

    r_k[2].wait_recv()
    r_k[3] = send(K.at[pl.ds(2 * T, T)], K.at[pl.ds(3 * T, T)], "sib")
    r_v[2].wait_recv()
    r_v[3] = send(V.at[pl.ds(2 * T, T)], V.at[pl.ds(3 * T, T)], "sib")

    l_low.wait()
    r_part.wait_recv()
    base = (PART[...].astype(F32) + PARTR[...].astype(F32)) * coef
    dlh = base[W:].astype(BF16)
    DOT[0, W:] = dlh
    DOT[0, :W] = (base[:W] + nn(LOW[...], dlh)).astype(BF16)
    r_do = ring("z", lambda d: DOT.at[0], lambda e: DOT.at[e])

    for cp in l_kv:
        cp.wait()
    for r in (1, 3):
        r_k[r].wait_recv()
        r_v[r].wait_recv()
    for h in range(NH):
        hs = slice(h * HD, (h + 1) * HD)
        KT[h] = K[:, hs].T
        VT[h] = V[:, hs].T

    l_q.wait()
    m2 = {}
    for d in (0, 1, 3, 2):
        if d:
            r_q[d].wait_recv()
            r_bias[d].wait_recv()
        bias = BIAS[4 + d] if d else BIAS[0]
        for h in range(NH):
            hs = slice(h * HD, (h + 1) * HD)
            sc = nt(K[:, hs], Q[d * T:(d + 1) * T, hs])
            sc = jnp.minimum(sc.reshape(8, 128, T), bias[:, None, :]).reshape(NK, T)
            top = jnp.max(sc, axis=0, keepdims=True) * C2
            p = jnp.exp2(sc * C2 - top)
            total = jnp.sum(p, axis=0, keepdims=True)
            pb = p.astype(BF16)
            PR[h, :, d * T:(d + 1) * T] = pb
            OT[h, d] = nn(VT[h], pb) / total
            STO[d, h:h + 1] = top + jnp.log2(total)
            m2[h, d] = top

    for d in (0, 1, 3, 2):
        if d:
            r_do[d].wait_recv()
        for h in range(NH):
            do = DOT[d, h * HD:(h + 1) * HD].astype(F32)
            STO[d, 3 + h:4 + h] = jnp.sum(do * OT[h, d], axis=0, keepdims=True)
        STO[d, 6:8] = jnp.zeros((2, T), F32)
    r_st = ring("z", lambda d: STO, lambda e: STR.at[e - 1])
    for e in (1, 3, 2):
        r_st[e].wait_recv()

    fac, delta = {}, {}
    slope = [jnp.zeros((RANK, HD), F32) for _ in range(NH)]
    for d in range(4):
        lh = jnp.zeros((RANK, T), F32)
        for h in range(NH):
            parts = [STO[d, h:h + 1]] + [STR[e - 1, (d - e) % 4, h:h + 1] for e in (1, 2, 3)]
            dels = [STO[d, 3 + h:4 + h]] + [STR[e - 1, (d - e) % 4, 3 + h:4 + h] for e in (1, 2, 3)]
            top = functools.reduce(jnp.maximum, parts)
            ws = [jnp.exp2(p - top) for p in parts]
            total = ws[0] + ws[1] + ws[2] + ws[3]
            fac[h, d] = jnp.exp2(m2[h, d] - top) / total
            delta[h, d] = (ws[0] * dels[0] + ws[1] * dels[1] + ws[2] * dels[2] + ws[3] * dels[3]) / total
            ob = (OT[h, d] * (ws[0] / total)).astype(BF16)
            low = LOW[h * HD:(h + 1) * HD]
            lh += lax.dot_general(low, ob, (((0,), (0,)), ((), ())), preferred_element_type=F32)
            slope[h] += nt(DOT[d, W:], ob)
        LHB[d] = (lh * coef).astype(BF16)
    r_lh = ring("z", lambda d: LHB.at[d], lambda e: LHR.at[e - 1])

    def attention_back(h):
        hs = slice(h * HD, (h + 1) * HD)
        dk = jnp.zeros((NK, HD), F32)
        dv = jnp.zeros((NK, HD), F32)
        for d in range(4):
            do = DOT[d, hs]
            dp = nn(V[:, hs], do)
            p = PR[h, :, d * T:(d + 1) * T].astype(F32) * fac[h, d]
            ds = (p * (dp - delta[h, d])).astype(BF16)
            dk += nn(ds, Q[d * T:(d + 1) * T, hs])
            dv += nt(p.astype(BF16), do)
            dq = nn(KT[h], ds) * SCALE
            DQB[h, d] = dq.astype(BF16)
            if d == 0:
                DQ0[h] = dq
        DK[h] = dk * SCALE
        DV[h] = dv
        DKB[h] = DK[h].astype(BF16)
        DVB[h] = dv.astype(BF16)
        r_dq[h] = ring("z", lambda d: DQB.at[h, d], lambda e: DQR.at[h, e - 1])
        for r in (3, 1):
            rows = pl.ds(r * T, T)
            i = 0 if r == 3 else 1
            r_dks[h, r] = send(DKB.at[h, rows], DKR.at[h, i], "sib")
            r_dvs[h, r] = send(DVB.at[h, rows], DVR.at[h, i], "sib")

    def cross(h):
        rows = slice(2 * T, 3 * T)
        r_dks[h, 3].wait_recv()
        DKX[h] = (DK[h, rows] + DKR[h, 0].astype(F32)).astype(BF16)
        r_dkx[h] = send(DKX.at[h], DKXR.at[h], "x")
        r_dvs[h, 3].wait_recv()
        DVX[h] = (DV[h, rows] + DVR[h, 0].astype(F32)).astype(BF16)
        r_dvx[h] = send(DVX.at[h], DVXR.at[h], "x")

    DQ0 = {}
    r_dq, r_dks, r_dvs, r_dkx, r_dvx = {}, {}, {}, {}, {}
    attention_back(0)

    for e in (1, 3, 2):
        r_lh[e].wait_recv()
    lhz = LHB[0].astype(F32) + LHR[0].astype(F32) + LHR[1].astype(F32) + LHR[2].astype(F32)
    LHY[...] = lhz.astype(BF16)
    r_lhy = ring("y", lambda d: LHY, lambda e: LHYR.at[e - 1])
    cross(0)
    attention_back(1)

    for e in (1, 3, 2):
        r_lhy[e].wait_recv()
    lhy = lhz + LHYR[0].astype(F32) + LHYR[1].astype(F32) + LHYR[2].astype(F32)
    LHC[...] = lhy.astype(BF16)
    r_lhc = send(LHC, LHCR, "cfg")
    cross(1)
    attention_back(2)

    r_lhc.wait_recv()
    lhs = (lhy + LHCR[...].astype(F32)).astype(BF16)
    gup = nn(lhs, COT[0])
    for t in range(4):
        GSB[t, 0:16] = gup[t * 16:(t + 1) * 16].astype(BF16)
        for h in range(NH):
            GSB[t, 16:32, h * HD:(h + 1) * HD] = slope[h][t * 16:(t + 1) * 16].astype(BF16)
    r_gs = ring("z", lambda d: GSB.at[(z + d) % 4], lambda e: GSR.at[e - 1])
    cross(2)

    for e in (1, 3, 2):
        r_gs[e].wait_recv()
    s1 = GSB[z].astype(F32) + GSR[0].astype(F32) + GSR[1].astype(F32) + GSR[2].astype(F32)
    S1B[...] = s1.astype(BF16)
    r_s1 = [send(S1B, S1R.at[i], to) for i, to in enumerate(("sib", "x", "xo"))]
    for cp in r_s1:
        cp.wait_recv()
    s2 = s1 + S1R[0].astype(F32) + S1R[1].astype(F32) + S1R[2].astype(F32)
    S2B[...] = s2.astype(BF16)
    r_s2 = send(S2B, S2R, "cfg")
    r_s2.wait_recv()
    GU[0, 0, c] = S2B[0:16]
    GU[0, 0, 1 - c] = S2R[0:16]
    SL[0] = (s2[16:32] + S2R[16:32].astype(F32)).astype(BF16)
    r_gu = ring("y", lambda d: GU.at[0, 0], lambda e: GU.at[0, e])
    for e in (1, 3, 2):
        r_gu[e].wait_recv()
    r_guz = ring("z", lambda d: GU.at[0], lambda e: GU.at[e])
    r_sl = ring("z", lambda d: SL.at[0], lambda e: SL.at[e])

    for h in range(NH):
        hs = slice(h * HD, (h + 1) * HD)
        dq = DQ0[h]
        for e in (1, 3, 2):
            r_dq[h][e].wait_recv()
            dq += DQR[h, e - 1].astype(F32)
        dq_out[:, hs] = dq.T.astype(BF16)
        for out, own, near, far, r_near, r_far in (
            (dk_out, DK, DKR, DKXR, r_dks, r_dkx),
            (dv_out, DV, DVR, DVXR, r_dvs, r_dvx),
        ):
            r_near[h, 1].wait_recv()
            r_far[h].wait_recv()
            out[:, hs] = (own[h, 0:T] + near[h, 1].astype(F32) + far[h].astype(F32)).astype(BF16)

    for e in (1, 3, 2):
        r_guz[e].wait_recv()
        r_sl[e].wait_recv()
    for d in range(4):
        rows = pl.ds(pl.multiple_of(((z + d) % 4) * 16, 16), 16)
        SLT[rows] = SL[d].astype(F32)
        for j in range(4):
            for b in range(2):
                col = pl.multiple_of((((hy + j) % 4) * 2 + b) * W, 128)
                gup_out[rows, pl.ds(col, W)] = GU[d, j, b].astype(F32)
    slope_out[...] = SLT[...].T
    for cp in started:
        cp.wait_send()


def scratch():
    v = pltpu.VMEM
    return [
        v((4 * T, W), BF16),
        v((NK, W), BF16),
        v((NK, W), BF16),
        v((NH, HD, NK), BF16),
        v((NH, HD, NK), BF16),
        v((4, T, W), BF16),
        v((4, W + RANK, W), BF16),
        v((W, RANK), BF16),
        v((W + RANK, T), BF16),
        v((W + RANK, T), BF16),
        v((4, W + RANK, T), BF16),
        v((8, 8, T), F32),
        v((NH, NK, 4 * T), BF16),
        v((NH, 4, HD, T), F32),
        v((4, 8, T), F32),
        v((3, 4, 8, T), F32),
        v((NH, NK, HD), F32),
        v((NH, NK, HD), F32),
        v((NH, 4, HD, T), BF16),
        v((NH, 3, HD, T), BF16),
        v((NH, NK, HD), BF16),
        v((NH, NK, HD), BF16),
        v((NH, 2, T, HD), BF16),
        v((NH, 2, T, HD), BF16),
        v((NH, T, HD), BF16),
        v((NH, T, HD), BF16),
        v((NH, T, HD), BF16),
        v((NH, T, HD), BF16),
        v((4, RANK, T), BF16),
        v((3, RANK, T), BF16),
        v((RANK, T), BF16),
        v((3, RANK, T), BF16),
        v((RANK, T), BF16),
        v((RANK, T), BF16),
        v((4, 32, W), BF16),
        v((3, 32, W), BF16),
        v((32, W), BF16),
        v((3, 32, W), BF16),
        v((32, W), BF16),
        v((32, W), BF16),
        v((4, 4, 2, 16, W), BF16),
        v((4, 16, W), BF16),
        v((RANK, W), F32),
        pltpu.SemaphoreType.DMA((NSEM,)),
        pltpu.SemaphoreType.DMA((NSEM,)),
        pltpu.SemaphoreType.DMA((16,)),
    ]


def per_device(query, key, value, cotangent, slots, counts, guidance, weight, lowering, raising):
    hbm = pl.BlockSpec(memory_space=pl.ANY)
    smem = pl.BlockSpec(memory_space=pltpu.SMEM)
    vmem = pl.BlockSpec(memory_space=pltpu.VMEM)
    dq, dk, dv, slope, gup = pl.pallas_call(
        kernel,
        out_shape=(
            jax.ShapeDtypeStruct((T, W), BF16),
            jax.ShapeDtypeStruct((T, W), BF16),
            jax.ShapeDtypeStruct((T, W), BF16),
            jax.ShapeDtypeStruct((W, RANK), F32),
            jax.ShapeDtypeStruct((RANK, 8 * W), F32),
        ),
        in_specs=[hbm] * 7 + [smem] * 3,
        out_specs=(vmem,) * 5,
        scratch_shapes=scratch(),
        compiler_params=pltpu.CompilerParams(
            collective_id=0, has_side_effects=True, vmem_limit_bytes=56 * 2 ** 20
        ),
        cost_estimate=pl.CostEstimate(flops=10**10, bytes_accessed=8 * 10**6, transcendentals=3 * 10**6),
    )(query[0], key[0], value[0], cotangent, weight, lowering, raising, slots, counts, guidance)
    return dq[None], dk[None], dv[None], slope, gup


def solution(mesh):
    in_specs = (
        P("cfg", "seq", "head"),
        P("cfg", "seq", "head"),
        P("cfg", "seq", "head"),
        P("seq", ("head", "cfg")),
        P("seq", None),
        P("seq"),
        P(),
        P("head", None),
        P("head", None),
        P(),
    )
    out_specs = (
        P("cfg", "seq", "head"),
        P("cfg", "seq", "head"),
        P("cfg", "seq", "head"),
        P("head", None),
        P(),
    )
    return jax.shard_map(
        per_device, mesh=mesh, in_specs=in_specs, out_specs=out_specs, check_vma=False
    )
```

```python
import functools
import math

import jax
import jax.numpy as jnp
from jax import lax
from jax.experimental import pallas as pl
from jax.experimental.pallas import tpu as pltpu
from jax.sharding import PartitionSpec as P

HD = 128
NH = 3
W = 384
T = 256
NK = 1024
RANK = 64
SCALE = HD ** -0.5
C2 = SCALE * math.log2(math.e)
BIG = 3.0e38
F32 = jnp.float32
BF16 = jnp.bfloat16
MESH = pl.DeviceIdType.MESH
NSEM = 112


def nn(a, b):
    return lax.dot_general(a, b, (((1,), (0,)), ((), ())), preferred_element_type=F32)


def nt(a, b):
    return lax.dot_general(a, b, (((1,), (1,)), ((), ())), preferred_element_type=F32)


def tn(a, b):
    return lax.dot_general(a, b, (((0,), (0,)), ((), ())), preferred_element_type=F32)


def kernel(
    q_in, k_in, v_in, cot_in, w_in, low_in, up_in, slots_ref, counts_ref, guide_ref,
    dq_out, dk_out, dv_out, slope_out, gup_out,
    Q, K, V, KT, VT, COT, WB, LOW, PART, PARTR, DOT, BIAS, PR, OT, STO, STR, DLO, DLR,
    DK, DV, DQ, DQB, DQR, DKB, DVB, DKR, DVR, DKX, DVX, DKXR, DVXR,
    LHB, LHR, LHY, LHYR, GSB, GSR, S1, GU, SL,
    send_sem, recv_sem, loc_sem,
):
    s, hy, c = lax.axis_index("seq"), lax.axis_index("head"), lax.axis_index("cfg")
    z, x, kc = s // 4, (s // 2) % 2, s % 2
    g = s % 4
    plane = {
        "sib": z * 4 + x * 2 + (1 - kc),
        "x": z * 4 + (1 - x) * 2 + kc,
        "xo": z * 4 + (1 - x) * 2 + (1 - kc),
    }
    peer = {"cfg": {"cfg": 1 - c}}
    for d in (1, 2, 3):
        peer["z%d" % d] = {"seq": ((z + d) % 4) * 4 + g}
        peer["y%d" % d] = {"head": (hy + d) % 4}
        peer["cy%d" % d] = {"head": (hy + d) % 4, "cfg": 1 - c}
    for name, at in plane.items():
        peer[name] = {"seq": at}
        peer["c" + name] = {"seq": at, "cfg": 1 - c}

    count = [0, 0]
    started = []

    def local(src, dst):
        cp = pltpu.make_async_copy(src, dst, loc_sem.at[count[1]])
        count[1] += 1
        cp.start()
        return cp

    def send(src, dst, to):
        i = count[0]
        count[0] += 1
        cp = pltpu.make_async_remote_copy(
            src_ref=src, dst_ref=dst, send_sem=send_sem.at[i], recv_sem=recv_sem.at[i],
            device_id=peer[to], device_id_type=MESH,
        )
        cp.start()
        started.append(cp)
        return cp

    def ring(axis, src, dst):
        got = {}
        for d in (1, 3, 2):
            e = (4 - d) % 4
            got[e] = send(src(d), dst(e), "%s%d" % (axis, d))
        return got

    l_cot = local(cot_in, COT.at[0])
    l_w = []
    for j in range(4):
        col = pl.multiple_of((((hy + j) % 4) * 2 + c) * W, 128)
        l_w.append(local(w_in.at[:, pl.ds(col, W)], WB.at[j, pl.ds(RANK, W)]))
        l_w.append(local(up_in.at[:, pl.ds(col, W)], WB.at[j, pl.ds(0, RANK)]))
    l_kv = [local(k_in, K.at[pl.ds(0, T)]), local(v_in, V.at[pl.ds(0, T)])]
    l_q = local(q_in, Q.at[pl.ds(0, T)])
    l_low = local(low_in, LOW)

    barrier = pltpu.get_barrier_semaphore()
    for name in peer:
        pl.semaphore_signal(barrier, inc=1, device_id=peer[name], device_id_type=MESH)
    pl.semaphore_wait(barrier, len(peer))

    r_cot = ring("y", lambda d: cot_in, lambda e: COT.at[e])
    r_k = {}
    r_v = {}
    for to, r in (("sib", 1), ("x", 2)):
        r_k[r] = send(k_in, K.at[pl.ds(r * T, T)], to)
        r_v[r] = send(v_in, V.at[pl.ds(r * T, T)], to)
    r_q = ring("z", lambda d: q_in, lambda e: Q.at[pl.ds(e * T, T)])

    row = lax.broadcasted_iota(jnp.int32, (8, T), 0)
    lane = lax.broadcasted_iota(jnp.int32, (8, T), 1)
    rx, rk = row // 4, (row // 2) % 2
    gx = x + rx - 2 * x * rx
    gk = kc + rk - 2 * kc * rk
    base_block = 2 * (gx * 2 + gk) + row % 2
    for d in range(4):
        block = base_block + 8 * ((z + d) % 4)
        live = jnp.zeros((8, T), F32)
        for qb in range(2):
            n = counts_ref[qb]
            for j in range(16):
                want = jnp.where(j < n, slots_ref[qb, j], -1)
                hit = jnp.logical_and(block == want, lane // 128 == qb)
                live = jnp.where(hit, 1.0, live)
        BIAS[d] = jnp.where(live > 0, BIG, -BIG)
    r_bias = ring("z", lambda d: BIAS.at[d], lambda e: BIAS.at[4 + e])

    weight = 1.5 + 0.5 * guide_ref[0].astype(F32)
    coef = jnp.where(c == 0, weight, 1.0 - weight)

    first = {}

    def forward(d, half):
        ks = slice(half * NK // 2, (half + 1) * NK // 2)
        bias = BIAS[4 + d] if d else BIAS[0]
        bias = bias[half * 4:half * 4 + 4]
        for h in range(NH):
            hs = slice(h * HD, (h + 1) * HD)
            sc = nt(K[ks, hs], Q[d * T:(d + 1) * T, hs])
            sc = jnp.minimum(sc.reshape(4, 128, T), bias[:, None, :]).reshape(NK // 2, T)
            top = jnp.max(sc, axis=0, keepdims=True) * C2
            p = jnp.exp2(sc * C2 - top)
            total = jnp.sum(p, axis=0, keepdims=True)
            pb = p.astype(BF16)
            PR[h, ks, d * T:(d + 1) * T] = pb
            o = nn(VT[h, :, ks], pb)
            if half == 0:
                OT[h, d] = o
                first[h, d] = (top, total)
            else:
                top0, total0 = first[h, d]
                m = jnp.maximum(top, top0)
                a0, a1 = jnp.exp2(top0 - m), jnp.exp2(top - m)
                total = total0 * a0 + total * a1
                inv = 1.0 / total
                OT[h, d] = OT[h, d] * (a0 * inv) + o * (a1 * inv)
                STO[d, h:h + 1] = m + jnp.log2(total)
                tops[h, d] = (top0, top)
        if half == 1:
            STO[d, NH:] = jnp.zeros((8 - NH, T), F32)

    tops = {}
    for cp in l_kv:
        cp.wait()
    l_q.wait()
    r_k[1].wait_recv()
    r_v[1].wait_recv()
    for h in range(NH):
        VT[h, :, :NK // 2] = V[:NK // 2, h * HD:(h + 1) * HD].T
    forward(0, 0)
    for d in (1, 3):
        r_q[d].wait_recv()
        r_bias[d].wait_recv()
        forward(d, 0)

    l_cot.wait()
    for cp in l_w:
        cp.wait()
    for e in (1, 3, 2):
        r_cot[e].wait_recv()
    bands = [slice(0, RANK + HD), slice(RANK + HD, RANK + 2 * HD), slice(RANK + 2 * HD, RANK + 3 * HD)]
    r_part = []
    for band in bands:
        acc = nt(WB[0, band], COT[0]) + nt(WB[1, band], COT[1]) + nt(WB[2, band], COT[2]) + nt(WB[3, band], COT[3])
        PART[band] = acc.astype(BF16)
        r_part.append(send(PART.at[band], PARTR.at[band], "cfg"))

    r_k[2].wait_recv()
    r_k[3] = send(K.at[pl.ds(2 * T, T)], K.at[pl.ds(3 * T, T)], "sib")
    r_v[2].wait_recv()
    r_v[3] = send(V.at[pl.ds(2 * T, T)], V.at[pl.ds(3 * T, T)], "sib")
    l_low.wait()
    r_k[3].wait_recv()
    r_v[3].wait_recv()
    for h in range(NH):
        VT[h, :, NK // 2:] = V[NK // 2:, h * HD:(h + 1) * HD].T

    r_do = []
    for h, d in enumerate((0, 1, 3)):
        forward(d, 1)
        band = bands[h]
        r_part[h].wait_recv()
        base = (PART[band].astype(F32) + PARTR[band].astype(F32)) * coef
        if h == 0:
            dlh = base[:RANK].astype(BF16)
            DOT[0, :RANK] = dlh
            base = base[RANK:]
        hs = slice(h * HD, (h + 1) * HD)
        DOT[0, RANK + h * HD:RANK + (h + 1) * HD] = (base + tn(LOW[:, hs], dlh)).astype(BF16)
        r_do.append(ring("z", lambda d: DOT.at[0, band], lambda e: DOT.at[e, band]))
    r_q[2].wait_recv()
    r_bias[2].wait_recv()
    forward(2, 0)
    forward(2, 1)
    r_st = ring("z", lambda d: STO, lambda e: STR.at[e - 1])
    for h in range(NH):
        KT[h] = K[:, h * HD:(h + 1) * HD].T

    r_dl = []

    def send_delta(h):
        for d in range(4):
            if d:
                r_do[h][d].wait_recv()
            do = DOT[d, RANK + h * HD:RANK + (h + 1) * HD].astype(F32)
            DLO[h, d:d + 1] = jnp.sum(do * OT[h, d], axis=0, keepdims=True)
        DLO[h, 4:] = jnp.zeros((4, T), F32)
        r_dl.append(ring("z", lambda d: DLO.at[h], lambda e: DLR.at[h, e - 1]))

    send_delta(0)

    for e in (1, 3, 2):
        r_st[e].wait_recv()
    fac, share = {}, {}
    slope = [jnp.zeros((RANK, HD), F32) for _ in range(NH)]
    for d in (1, 3, 2, 0):
        lh = jnp.zeros((RANK, T), F32)
        for h in range(NH):
            parts = [STO[d, h:h + 1]] + [STR[e - 1, (d - e) % 4, h:h + 1] for e in (1, 2, 3)]
            top = functools.reduce(jnp.maximum, parts)
            ws = [jnp.exp2(p - top) for p in parts]
            inv = 1.0 / (ws[0] + ws[1] + ws[2] + ws[3])
            share[h, d] = [w * inv for w in ws]
            fac[h, d] = [jnp.exp2(m - top) * inv for m in tops[h, d]]
            ob = (OT[h, d] * share[h, d][0]).astype(BF16)
            lh += nn(LOW[:, h * HD:(h + 1) * HD], ob)
            slope[h] += nt(DOT[d, :RANK], ob)
        LHB[d] = (lh * coef).astype(BF16)
    r_lh = ring("z", lambda d: LHB.at[d], lambda e: LHR.at[e - 1])

    delta = {}

    def get_delta(h):
        for e in (1, 3, 2):
            r_dl[h][e].wait_recv()
        for d in range(4):
            dels = [DLO[h, d:d + 1]] + [DLR[h, e - 1, (d - e) % 4:(d - e) % 4 + 1] for e in (1, 2, 3)]
            delta[h, d] = functools.reduce(lambda a, b: a + b, [w * v for w, v in zip(share[h, d], dels)])

    r_dq, r_dks, r_dvs, r_dkx, r_dvx = {}, {}, {}, {}, {}

    def back(h, d):
        hs = slice(h * HD, (h + 1) * HD)
        qs = slice(d * T, (d + 1) * T)
        do = DOT[d, RANK + h * HD:RANK + (h + 1) * HD]
        dp = nn(V[:, hs], do)
        near = PR[h, :NK // 2, qs].astype(F32) * fac[h, d][0]
        far = PR[h, NK // 2:, qs].astype(F32) * fac[h, d][1]
        p = jnp.concatenate([near, far], axis=0)
        ds = (p * (dp - delta[h, d])).astype(BF16)
        dk = nn(ds, Q[d * T:(d + 1) * T, hs]) * SCALE
        dv = nt(p.astype(BF16), do)
        dq = nn(KT[h], ds) * SCALE
        if d == 0:
            DQ[h] = dq
        else:
            DQB[h, d] = dq.astype(BF16)
            r_dq[h, (4 - d) % 4] = send(DQB.at[h, d], DQR.at[h, 3 - d], "z%d" % d)
        return dk, dv

    def head_done(h, dk, dv):
        DK[h] = dk
        DV[h] = dv
        DKB[h] = dk.astype(BF16)
        DVB[h] = dv.astype(BF16)
        for r in (3, 1):
            rows = pl.ds(r * T, T)
            i = 0 if r == 3 else 1
            r_dks[h, r] = send(DKB.at[h, rows], DKR.at[h, i], "sib")
            r_dvs[h, r] = send(DVB.at[h, rows], DVR.at[h, i], "sib")

    def cross(h):
        rows = slice(2 * T, 3 * T)
        r_dks[h, 3].wait_recv()
        DKX[h] = (DK[h, rows] + DKR[h, 0].astype(F32)).astype(BF16)
        r_dkx[h] = send(DKX.at[h], DKXR.at[h], "x")
        r_dvs[h, 3].wait_recv()
        DVX[h] = (DV[h, rows] + DVR[h, 0].astype(F32)).astype(BF16)
        r_dvx[h] = send(DVX.at[h], DVXR.at[h], "x")

    def finish(h):
        hs = slice(h * HD, (h + 1) * HD)
        dq = DQ[h]
        for e in (1, 3, 2):
            r_dq[h, e].wait_recv()
            dq += DQR[h, e - 1].astype(F32)
        dq_out[:, hs] = dq.T.astype(BF16)
        for out, own, near, far, r_near, r_far in (
            (dk_out, DK, DKR, DKXR, r_dks, r_dkx),
            (dv_out, DV, DVR, DVXR, r_dvs, r_dvx),
        ):
            r_near[h, 1].wait_recv()
            r_far[h].wait_recv()
            out[:, hs] = (own[h, 0:T] + near[h, 1].astype(F32) + far[h].astype(F32)).astype(BF16)

    chain = {}

    def chain_lh():
        for e in (1, 3, 2):
            r_lh[e].wait_recv()
        lhz = LHB[0].astype(F32) + LHR[0].astype(F32) + LHR[1].astype(F32) + LHR[2].astype(F32)
        chain["lhz"] = lhz
        LHY[...] = lhz.astype(BF16)
        names = ("y1", "y3", "y2", "cfg", "cy1", "cy3", "cy2")
        chain["lhy"] = [send(LHY, LHYR.at[i], to) for i, to in enumerate(names)]

    def chain_gup():
        lhs = chain["lhz"]
        for i, cp in enumerate(chain["lhy"]):
            cp.wait_recv()
            lhs += LHYR[i].astype(F32)
        gup = nn(lhs.astype(BF16), COT[0])
        for t in range(4):
            GSB[t, 0:16] = gup[t * 16:(t + 1) * 16].astype(BF16)
            for h in range(NH):
                GSB[t, 16:32, h * HD:(h + 1) * HD] = slope[h][t * 16:(t + 1) * 16].astype(BF16)
        chain["gs"] = ring("z", lambda d: GSB.at[(z + d) % 4], lambda e: GSR.at[e - 1])

    def chain_plane():
        for e in (1, 3, 2):
            chain["gs"][e].wait_recv()
        s1 = GSB[z].astype(F32) + GSR[0].astype(F32) + GSR[1].astype(F32) + GSR[2].astype(F32)
        S1[c, g] = s1.astype(BF16)
        names = ("sib", "x", "xo", "cfg", "csib", "cx", "cxo")
        chain["s1"] = [send(S1.at[c, g], S1.at[c, g], to) for to in names]

    def chain_y():
        for cp in chain["s1"]:
            cp.wait_recv()
        both = []
        for b in range(2):
            both.append(S1[b, 0].astype(F32) + S1[b, 1].astype(F32) + S1[b, 2].astype(F32) + S1[b, 3].astype(F32))
            GU[0, 0, b] = both[b][0:16].astype(BF16)
        SL[0] = (both[0][16:32] + both[1][16:32]).astype(BF16)
        chain["gu"] = ring("y", lambda d: GU.at[0, 0], lambda e: GU.at[0, e])
        chain["sl"] = ring("z", lambda d: SL.at[0], lambda e: SL.at[e])

    def chain_z():
        for e in (1, 3, 2):
            chain["gu"][e].wait_recv()
        chain["guz"] = ring("z", lambda d: GU.at[0], lambda e: GU.at[e])

    def chain_end():
        for e in (1, 3, 2):
            chain["guz"][e].wait_recv()
            chain["sl"][e].wait_recv()
        for d in range(4):
            rows = pl.ds(pl.multiple_of(((z + d) % 4) * 16, 16), 16)
            slope_out[rows] = SL[d].astype(F32)
            for j in range(4):
                for b in range(2):
                    col = pl.multiple_of((((hy + j) % 4) * 2 + b) * W, 128)
                    gup_out[rows, pl.ds(col, W)] = GU[d, j, b].astype(F32)

    send_delta(1)
    get_delta(0)
    hooks = {
        (0, 1): [chain_lh],
        (0, 2): [lambda: send_delta(2)],
        (0, 3): [chain_gup, lambda: get_delta(1)],
        (1, 1): [lambda: cross(0), chain_plane],
        (1, 3): [lambda: get_delta(2)],
        (2, 0): [chain_y],
        (2, 1): [lambda: cross(1)],
        (2, 3): [chain_z],
    }
    for h in range(NH):
        dk, dv = None, None
        for step, d in enumerate((1, 3, 2, 0)):
            a, b = back(h, d)
            dk = a if dk is None else dk + a
            dv = b if dv is None else dv + b
            if step == 3:
                head_done(h, dk, dv)
            for hook in hooks.get((h, step), []):
                hook()
    finish(0)
    cross(2)
    finish(1)
    chain_end()
    finish(2)
    for cp in started:
        cp.wait_send()


def hand_over(*refs):
    n = len(refs) // 2
    for i in range(n):
        refs[n + i][...] = refs[i][...]


def scratch():
    v = pltpu.VMEM
    return [
        v((4 * T, W), BF16),
        v((NK, W), BF16),
        v((NK, W), BF16),
        v((NH, HD, NK), BF16),
        v((NH, HD, NK), BF16),
        v((4, T, W), BF16),
        v((4, W + RANK, W), BF16),
        v((RANK, W), BF16),
        v((W + RANK, T), BF16),
        v((W + RANK, T), BF16),
        v((4, W + RANK, T), BF16),
        v((8, 8, T), F32),
        v((NH, NK, 4 * T), BF16),
        v((NH, 4, HD, T), F32),
        v((4, 8, T), F32),
        v((3, 4, 8, T), F32),
        v((NH, 8, T), F32),
        v((NH, 3, 8, T), F32),
        v((NH, NK, HD), F32),
        v((NH, NK, HD), F32),
        v((NH, HD, T), F32),
        v((NH, 4, HD, T), BF16),
        v((NH, 3, HD, T), BF16),
        v((NH, NK, HD), BF16),
        v((NH, NK, HD), BF16),
        v((NH, 2, T, HD), BF16),
        v((NH, 2, T, HD), BF16),
        v((NH, T, HD), BF16),
        v((NH, T, HD), BF16),
        v((NH, T, HD), BF16),
        v((NH, T, HD), BF16),
        v((4, RANK, T), BF16),
        v((3, RANK, T), BF16),
        v((RANK, T), BF16),
        v((7, RANK, T), BF16),
        v((4, 32, W), BF16),
        v((3, 32, W), BF16),
        v((2, 4, 32, W), BF16),
        v((4, 4, 2, 16, W), BF16),
        v((4, 16, W), BF16),
        pltpu.SemaphoreType.DMA((NSEM,)),
        pltpu.SemaphoreType.DMA((NSEM,)),
        pltpu.SemaphoreType.DMA((16,)),
    ]


def per_device(query, key, value, cotangent, slots, counts, guidance, weight, lowering, raising):
    hbm = pl.BlockSpec(memory_space=pl.ANY)
    smem = pl.BlockSpec(memory_space=pltpu.SMEM)
    vmem = pl.BlockSpec(memory_space=pltpu.VMEM)
    shapes = (
        jax.ShapeDtypeStruct((T, W), BF16),
        jax.ShapeDtypeStruct((T, W), BF16),
        jax.ShapeDtypeStruct((T, W), BF16),
        jax.ShapeDtypeStruct((RANK, W), F32),
        jax.ShapeDtypeStruct((RANK, 8 * W), F32),
    )
    parts = pl.pallas_call(
        kernel,
        out_shape=shapes,
        in_specs=[hbm] * 7 + [smem] * 3,
        out_specs=(vmem,) * 5,
        scratch_shapes=scratch(),
        compiler_params=pltpu.CompilerParams(
            collective_id=0, has_side_effects=True, vmem_limit_bytes=56 * 2 ** 20
        ),
        cost_estimate=pl.CostEstimate(flops=10**10, bytes_accessed=8 * 10**6, transcendentals=3 * 10**6),
    )(query[0], key[0], value[0], cotangent, weight, lowering.T, raising, slots, counts, guidance)
    dq, dk, dv, slope, gup = pl.pallas_call(
        hand_over,
        out_shape=shapes,
        in_specs=[vmem] * 5,
        out_specs=(vmem,) * 5,
        cost_estimate=pl.CostEstimate(flops=0, bytes_accessed=4 * 10**6, transcendentals=0),
    )(*parts)
    return dq[None], dk[None], dv[None], slope.T, gup


def solution(mesh):
    in_specs = (
        P("cfg", "seq", "head"),
        P("cfg", "seq", "head"),
        P("cfg", "seq", "head"),
        P("seq", ("head", "cfg")),
        P("seq", None),
        P("seq"),
        P(),
        P("head", None),
        P("head", None),
        P(),
    )
    out_specs = (
        P("cfg", "seq", "head"),
        P("cfg", "seq", "head"),
        P("cfg", "seq", "head"),
        P("head", None),
        P(),
    )
    return jax.shard_map(
        per_device, mesh=mesh, in_specs=in_specs, out_specs=out_specs, check_vma=False
    )
```

```python
import functools
import math

import jax
import jax.numpy as jnp
from jax import lax
from jax.experimental import pallas as pl
from jax.experimental.pallas import tpu as pltpu
from jax.sharding import PartitionSpec as P

HD = 128
NH = 3
W = 384
T = 256
NK = 1024
RANK = 64
SCALE = HD ** -0.5
C2 = SCALE * math.log2(math.e)
BIG = 3.0e38
F32 = jnp.float32
BF16 = jnp.bfloat16
MESH = pl.DeviceIdType.MESH
NSEM = 128


def nn(a, b):
    return lax.dot_general(a, b, (((1,), (0,)), ((), ())), preferred_element_type=F32)


def nt(a, b):
    return lax.dot_general(a, b, (((1,), (1,)), ((), ())), preferred_element_type=F32)


def tn(a, b):
    return lax.dot_general(a, b, (((0,), (0,)), ((), ())), preferred_element_type=F32)


def kernel(
    q_in, k_in, v_in, cot_in, w_in, low_in, up_in, slots_ref, counts_ref, guide_ref,
    dq_out, dk_out, dv_out, slope_out, gup_out,
    Q, K, V, KT, VT, COT, WB, LOW, PART, PARTR, DOT, BIAS, PR, OT, STO, STR, DLO, DLR,
    DK, DV, DQ, DQB, DQR, DKB, DVB, DKR, DVR, DKX, DVX, DKXR, DVXR,
    LHB, LHR, LHO, LHY, LHYR, GSB, GSR, S1, GU, SL,
    send_sem, recv_sem, loc_sem,
):
    s, hy, c = lax.axis_index("seq"), lax.axis_index("head"), lax.axis_index("cfg")
    z, x, kc = s // 4, (s // 2) % 2, s % 2
    g = s % 4
    px = [x, x, 1 - x, 1 - x]
    pk = [kc, 1 - kc, kc, 1 - kc]
    peer = {"cfg": {"cfg": 1 - c}}
    for r in range(4):
        for d in range(4):
            if r or d:
                peer["s%d%d" % (d, r)] = {"seq": ((z + d) % 4) * 4 + px[r] * 2 + pk[r]}
        if r:
            peer["c%d" % r] = {"seq": z * 4 + px[r] * 2 + pk[r], "cfg": 1 - c}
    for d in (1, 2, 3):
        peer["y%d" % d] = {"head": (hy + d) % 4}
        peer["cy%d" % d] = {"head": (hy + d) % 4, "cfg": 1 - c}
        for t in (1, 2, 3):
            peer["yz%d%d" % (d, t)] = {"head": (hy + d) % 4, "seq": ((z + t) % 4) * 4 + g}
    for name, alias in (("sib", "s01"), ("x", "s02"), ("xo", "s03"), ("z1", "s10"), ("z2", "s20"), ("z3", "s30")):
        peer[name] = peer[alias]
    everyone = [name for name in peer if name not in ("sib", "x", "xo", "z1", "z2", "z3")]

    count = [0, 0]
    started = []

    def local(src, dst):
        cp = pltpu.make_async_copy(src, dst, loc_sem.at[count[1]])
        count[1] += 1
        cp.start()
        return cp

    def send(src, dst, to):
        i = count[0]
        count[0] += 1
        cp = pltpu.make_async_remote_copy(
            src_ref=src, dst_ref=dst, send_sem=send_sem.at[i], recv_sem=recv_sem.at[i],
            device_id=peer[to], device_id_type=MESH,
        )
        cp.start()
        started.append(cp)
        return cp

    def ring(axis, src, dst):
        got = {}
        for d in (1, 3, 2):
            e = (4 - d) % 4
            got[e] = send(src(d), dst(e), "%s%d" % (axis, d))
        return got

    l_cot = local(cot_in, COT.at[0])
    l_w = []
    for j in range(4):
        col = pl.multiple_of((((hy + j) % 4) * 2 + c) * W, 128)
        l_w.append(local(w_in.at[:, pl.ds(col, W)], WB.at[j, pl.ds(RANK, W)]))
        l_w.append(local(up_in.at[:, pl.ds(col, W)], WB.at[j, pl.ds(0, RANK)]))
    l_kv = [local(k_in, K.at[pl.ds(0, T)]), local(v_in, V.at[pl.ds(0, T)])]
    l_q = local(q_in, Q.at[pl.ds(0, T)])
    l_low = local(low_in, LOW)

    barrier = pltpu.get_barrier_semaphore()
    for name in everyone:
        pl.semaphore_signal(barrier, inc=1, device_id=peer[name], device_id_type=MESH)
    pl.semaphore_wait(barrier, len(everyone))

    r_cot = ring("y", lambda d: cot_in, lambda e: COT.at[e])
    r_k = {}
    r_v = {}
    for to, r in (("sib", 1), ("x", 2)):
        r_k[r] = send(k_in, K.at[pl.ds(r * T, T)], to)
        r_v[r] = send(v_in, V.at[pl.ds(r * T, T)], to)
    r_q = {4 - d: send(q_in, Q.at[pl.ds((4 - d) * T, T)], "z%d" % d) for d in (1, 3)}

    row = lax.broadcasted_iota(jnp.int32, (8, T), 0)
    lane = lax.broadcasted_iota(jnp.int32, (8, T), 1)
    rx, rk = row // 4, (row // 2) % 2
    gx = x + rx - 2 * x * rx
    gk = kc + rk - 2 * kc * rk
    base_block = 2 * (gx * 2 + gk) + row % 2
    for d in range(4):
        block = base_block + 8 * ((z + d) % 4)
        live = jnp.zeros((8, T), F32)
        for qb in range(2):
            n = counts_ref[qb]
            for j in range(16):
                want = jnp.where(j < n, slots_ref[qb, j], -1)
                hit = jnp.logical_and(block == want, lane // 128 == qb)
                live = jnp.where(hit, 1.0, live)
        BIAS[d] = jnp.where(live > 0, BIG, -BIG)
    r_bias = ring("z", lambda d: BIAS.at[d], lambda e: BIAS.at[4 + e])

    weight = 1.5 + 0.5 * guide_ref[0].astype(F32)
    coef = jnp.where(c == 0, weight, 1.0 - weight)

    first = {}

    def forward(d, half):
        ks = slice(half * NK // 2, (half + 1) * NK // 2)
        bias = BIAS[4 + d] if d else BIAS[0]
        bias = bias[half * 4:half * 4 + 4]
        for h in range(NH):
            hs = slice(h * HD, (h + 1) * HD)
            sc = nt(K[ks, hs], Q[d * T:(d + 1) * T, hs])
            sc = jnp.minimum(sc.reshape(4, 128, T), bias[:, None, :]).reshape(NK // 2, T)
            top = jnp.max(sc, axis=0, keepdims=True) * C2
            p = jnp.exp2(sc * C2 - top)
            total = jnp.sum(p, axis=0, keepdims=True)
            pb = p.astype(BF16)
            PR[h, ks, d * T:(d + 1) * T] = pb
            o = nn(VT[h, :, ks], pb)
            if half == 0:
                OT[h, d] = o
                first[h, d] = (top, total)
            else:
                top0, total0 = first[h, d]
                m = jnp.maximum(top, top0)
                a0, a1 = jnp.exp2(top0 - m), jnp.exp2(top - m)
                total = total0 * a0 + total * a1
                inv = 1.0 / total
                OT[h, d] = OT[h, d] * (a0 * inv) + o * (a1 * inv)
                STO[4 * h + d:4 * h + d + 1] = m + jnp.log2(total)
                tops[h, d] = (top0, top)
                low = nn(LOW[:, hs], OT[h, d].astype(BF16))
                if d:
                    LHB[d, h * RANK:(h + 1) * RANK] = low.astype(BF16)
                else:
                    LHO[h] = low
        if half and d:
            r_lh[(4 - d) % 4] = send(LHB.at[d], LHR.at[3 - d], "z%d" % d)

    tops, r_lh = {}, {}
    for cp in l_kv:
        cp.wait()
    l_q.wait()
    r_k[1].wait_recv()
    r_v[1].wait_recv()
    for h in range(NH):
        VT[h, :, :NK // 2] = V[:NK // 2, h * HD:(h + 1) * HD].T
    forward(0, 0)
    for d in (1, 3):
        r_q[d].wait_recv()
    far_q = [
        send(Q.at[pl.ds(3 * T, T // 2)], Q.at[pl.ds(2 * T, T // 2)], "z1"),
        send(Q.at[pl.ds(T + T // 2, T // 2)], Q.at[pl.ds(2 * T + T // 2, T // 2)], "z3"),
    ]
    for d in (1, 3):
        r_bias[d].wait_recv()
        forward(d, 0)
    for cp in far_q:
        cp.wait_recv()
    r_bias[2].wait_recv()
    forward(2, 0)

    l_cot.wait()
    for cp in l_w:
        cp.wait()
    for e in (1, 3, 2):
        r_cot[e].wait_recv()
    r_k[2].wait_recv()
    r_k[3] = send(K.at[pl.ds(2 * T, T)], K.at[pl.ds(3 * T, T)], "sib")
    r_v[2].wait_recv()
    r_v[3] = send(V.at[pl.ds(2 * T, T)], V.at[pl.ds(3 * T, T)], "sib")
    bands = [slice(0, RANK + HD), slice(RANK + HD, RANK + 2 * HD), slice(RANK + 2 * HD, RANK + 3 * HD)]
    r_part = []
    for band in bands:
        acc = nt(WB[0, band], COT[0]) + nt(WB[1, band], COT[1]) + nt(WB[2, band], COT[2]) + nt(WB[3, band], COT[3])
        PART[band] = acc.astype(BF16)
        r_part.append(send(PART.at[band], PARTR.at[band], "cfg"))

    r_k[3].wait_recv()
    r_v[3].wait_recv()
    for h in range(NH):
        VT[h, :, NK // 2:] = V[NK // 2:, h * HD:(h + 1) * HD].T

    l_low.wait()
    r_do = []

    def send_do(h):
        band = bands[h]
        r_part[h].wait_recv()
        base = (PART[band].astype(F32) + PARTR[band].astype(F32)) * coef
        if h == 0:
            DOT[0, :RANK] = base[:RANK].astype(BF16)
            base = base[RANK:]
        hs = slice(h * HD, (h + 1) * HD)
        DOT[0, RANK + h * HD:RANK + (h + 1) * HD] = (base + tn(LOW[:, hs], DOT[0, :RANK])).astype(BF16)
        r_do.append({4 - d: send(DOT.at[0, band], DOT.at[4 - d, band], "z%d" % d) for d in (1, 3)})

    forward(2, 1)
    forward(1, 1)
    send_do(0)
    forward(3, 1)
    send_do(1)
    forward(0, 1)
    STO[4 * NH:] = jnp.zeros((16 - 4 * NH, T), F32)
    r_st = ring("z", lambda d: STO, lambda e: STR.at[e - 1])
    send_do(2)
    for h in range(NH):
        KT[h] = K[:, h * HD:(h + 1) * HD].T

    r_dl = []

    def relay_do(h):
        lo, n = bands[h].start, bands[h].stop - bands[h].start
        one = pl.ds(lo, n // 2)
        two = pl.ds(lo + n // 2, n // 2)
        r_do[h][3].wait_recv()
        a = send(DOT.at[3, one], DOT.at[2, one], "z1")
        r_do[h][1].wait_recv()
        b = send(DOT.at[1, two], DOT.at[2, two], "z3")
        r_do[h][2] = [a, b]

    def send_delta(h):
        for d in (0, 1, 3, 2):
            if d == 2:
                for cp in r_do[h][2]:
                    cp.wait_recv()
            do = DOT[d, RANK + h * HD:RANK + (h + 1) * HD].astype(F32)
            DLO[h, d:d + 1] = jnp.sum(do * OT[h, d], axis=0, keepdims=True)
        DLO[h, 4:] = jnp.zeros((4, T), F32)
        r_dl.append(ring("z", lambda d: DLO.at[h], lambda e: DLR.at[h, e - 1]))

    relay_do(0)
    for e in (1, 3, 2):
        r_st[e].wait_recv()
    fac, share = {}, {}
    for d in (0, 1, 3, 2):
        for h in range(NH):
            parts = [STO[4 * h + d:4 * h + d + 1]]
            for e in (1, 2, 3):
                i = 4 * h + (d - e) % 4
                parts.append(STR[e - 1, i:i + 1])
            top = functools.reduce(jnp.maximum, parts)
            ws = [jnp.exp2(p - top) for p in parts]
            inv = 1.0 / (ws[0] + ws[1] + ws[2] + ws[3])
            share[h, d] = [w * inv for w in ws]
            fac[h, d] = [jnp.exp2(m - top) * inv for m in tops[h, d]]
        if d == 0:
            lhz = functools.reduce(lambda a, b: a + b, [LHO[h] * share[h, 0][0] for h in range(NH)])
            for e in (1, 3, 2):
                r_lh[e].wait_recv()
                for h in range(NH):
                    lhz += LHR[e - 1, h * RANK:(h + 1) * RANK].astype(F32) * share[h, 0][e]
            lhz = lhz * coef
            LHY[...] = lhz.astype(BF16)
            names = ("y1", "y3", "y2", "cfg", "cy1", "cy3", "cy2")
            r_lhy = [send(LHY, LHYR.at[i], to) for i, to in enumerate(names)]
    relay_do(1)
    send_delta(0)
    relay_do(2)
    slope = [jnp.zeros((RANK, HD), F32) for _ in range(NH)]
    for d in (0, 1, 3, 2):
        for h in range(NH):
            slope[h] += nt(DOT[d, :RANK], (OT[h, d] * share[h, d][0]).astype(BF16))

    delta = {}

    def get_delta(h):
        for e in (1, 3, 2):
            r_dl[h][e].wait_recv()
        for d in range(4):
            dels = [DLO[h, d:d + 1]] + [DLR[h, e - 1, (d - e) % 4:(d - e) % 4 + 1] for e in (1, 2, 3)]
            delta[h, d] = functools.reduce(lambda a, b: a + b, [w * v for w, v in zip(share[h, d], dels)])

    r_dq, r_dks, r_dvs, r_dkx, r_dvx = {}, {}, {}, {}, {}

    def back(h, half, d):
        hs = slice(h * HD, (h + 1) * HD)
        ks = slice(half * NK // 2, (half + 1) * NK // 2)
        qs = slice(d * T, (d + 1) * T)
        do = DOT[d, RANK + h * HD:RANK + (h + 1) * HD]
        dp = nn(V[ks, hs], do)
        p = PR[h, ks, qs].astype(F32) * fac[h, d][half]
        ds = (p * (dp - delta[h, d])).astype(BF16)
        dk = nn(ds, Q[qs, hs]) * SCALE
        dv = nt(p.astype(BF16), do)
        dq = nn(KT[h, :, ks], ds) * SCALE
        if half == 1:
            DQ[h, d] = dq
        else:
            dq += DQ[h, d]
            if d == 0:
                DQ[h, 0] = dq
            else:
                DQB[h, d] = dq.astype(BF16)
                r_dq[h, (4 - d) % 4] = send(DQB.at[h, d], DQR.at[h, 3 - d], "z%d" % d)
        return dk, dv

    def half_done(h, half, dk, dv):
        ks = slice(half * NK // 2, (half + 1) * NK // 2)
        DK[h, ks] = dk
        DV[h, ks] = dv
        r = 1 + 2 * half
        DKB[h, half] = dk[T:].astype(BF16)
        DVB[h, half] = dv[T:].astype(BF16)
        r_dks[h, r] = send(DKB.at[h, half], DKR.at[h, 1 - half], "sib")
        r_dvs[h, r] = send(DVB.at[h, half], DVR.at[h, 1 - half], "sib")

    def cross(h):
        rows = slice(2 * T, 3 * T)
        r_dks[h, 3].wait_recv()
        DKX[h] = (DK[h, rows] + DKR[h, 0].astype(F32)).astype(BF16)
        r_dkx[h] = send(DKX.at[h], DKXR.at[h], "x")
        r_dvs[h, 3].wait_recv()
        DVX[h] = (DV[h, rows] + DVR[h, 0].astype(F32)).astype(BF16)
        r_dvx[h] = send(DVX.at[h], DVXR.at[h], "x")

    def finish(h):
        hs = slice(h * HD, (h + 1) * HD)
        dq = DQ[h, 0]
        for e in (1, 3, 2):
            r_dq[h, e].wait_recv()
            dq += DQR[h, e - 1].astype(F32)
        dq_out[:, hs] = dq.T.astype(BF16)
        for out, own, near, far, r_near, r_far in (
            (dk_out, DK, DKR, DKXR, r_dks, r_dkx),
            (dv_out, DV, DVR, DVXR, r_dvs, r_dvx),
        ):
            r_near[h, 1].wait_recv()
            r_far[h].wait_recv()
            out[:, hs] = (own[h, 0:T] + near[h, 1].astype(F32) + far[h].astype(F32)).astype(BF16)

    chain = {}

    def chain_gup():
        lhs = lhz
        for i, cp in enumerate(r_lhy):
            cp.wait_recv()
            lhs += LHYR[i].astype(F32)
        gup = nn(lhs.astype(BF16), COT[0])
        for t in range(16):
            GSB[t, 0:4] = gup[t * 4:(t + 1) * 4]
            for h in range(NH):
                GSB[t, 4:8, h * HD:(h + 1) * HD] = slope[h][t * 4:(t + 1) * 4]
        chain["gs"] = []
        for d in (1, 3, 2, 0):
            for r in range(4):
                if r or d:
                    i = ((4 - d) % 4) * 4 + r
                    to = ((z + d) % 4) * 4 + px[r] * 2 + pk[r]
                    chain["gs"].append(send(GSB.at[to], GSR.at[i], "s%d%d" % (d, r)))

    def chain_plane():
        for cp in chain["gs"]:
            cp.wait_recv()
        s1 = GSB[s]
        for i in range(1, 16):
            s1 += GSR[i]
        S1[c, g] = s1
        names = ("sib", "x", "xo", "cfg", "c1", "c2", "c3")
        chain["s1"] = [send(S1.at[c, g], S1.at[c, g], to) for to in names]

    def chain_yz():
        for cp in chain["s1"]:
            cp.wait_recv()
        for b in range(2):
            GU[0, 0, b] = jnp.concatenate([S1[b, i, 0:4] for i in range(4)], axis=0).astype(BF16)
        SL[0] = jnp.concatenate([S1[0, i, 4:8] + S1[1, i, 4:8] for i in range(4)], axis=0).astype(BF16)
        chain["sl"] = ring("z", lambda d: SL.at[0], lambda e: SL.at[e])
        chain["gu"] = ring("y", lambda d: GU.at[0, 0], lambda e: GU.at[0, e])
        chain["guz"] = ring("z", lambda d: GU.at[0, 0], lambda e: GU.at[e, 0])
        for d in (1, 3, 2):
            for t in (1, 3, 2):
                cp = send(GU.at[0, 0], GU.at[4 - t, 4 - d], "yz%d%d" % (d, t))
                chain["gu"][4 * d + t] = cp

    def chain_end():
        for cp in chain["gu"].values():
            cp.wait_recv()
        for e in (1, 3, 2):
            chain["guz"][e].wait_recv()
            chain["sl"][e].wait_recv()
        for d in range(4):
            rows = pl.ds(pl.multiple_of(((z + d) % 4) * 16, 16), 16)
            slope_out[rows] = SL[d].astype(F32)
            for j in range(4):
                for b in range(2):
                    col = pl.multiple_of((((hy + j) % 4) * 2 + b) * W, 128)
                    gup_out[rows, pl.ds(col, W)] = GU[d, j, b].astype(F32)

    get_delta(0)
    hooks = {
        (0, 1, 1): [lambda: send_delta(1), chain_gup],
        (0, 1, 3): [lambda: send_delta(2)],
        (0, 0, 1): [lambda: cross(0)],
        (0, 0, 3): [lambda: get_delta(1)],
        (1, 1, 3): [chain_plane],
        (1, 0, 1): [lambda: cross(1)],
        (1, 0, 3): [lambda: get_delta(2)],
        (2, 1, 3): [chain_yz],
        (2, 0, 1): [lambda: cross(2)],
    }
    for h in range(NH):
        for half in (1, 0):
            dk, dv = None, None
            for step, d in enumerate((1, 3, 2, 0)):
                a, b = back(h, half, d)
                dk = a if dk is None else dk + a
                dv = b if dv is None else dv + b
                if step == 3:
                    half_done(h, half, dk, dv)
                for hook in hooks.get((h, half, step), []):
                    hook()
    finish(0)
    finish(1)
    finish(2)
    chain_end()
    for cp in started:
        cp.wait_send()


def hand_over(*refs):
    n = len(refs) // 2
    for i in range(n):
        refs[n + i][...] = refs[i][...]


def scratch():
    v = pltpu.VMEM
    return [
        v((4 * T, W), BF16),
        v((NK, W), BF16),
        v((NK, W), BF16),
        v((NH, HD, NK), BF16),
        v((NH, HD, NK), BF16),
        v((4, T, W), BF16),
        v((4, W + RANK, W), BF16),
        v((RANK, W), BF16),
        v((W + RANK, T), BF16),
        v((W + RANK, T), BF16),
        v((4, W + RANK, T), BF16),
        v((8, 8, T), F32),
        v((NH, NK, 4 * T), BF16),
        v((NH, 4, HD, T), F32),
        v((16, T), F32),
        v((3, 16, T), F32),
        v((NH, 8, T), F32),
        v((NH, 3, 8, T), F32),
        v((NH, NK, HD), F32),
        v((NH, NK, HD), F32),
        v((NH, 4, HD, T), F32),
        v((NH, 4, HD, T), BF16),
        v((NH, 3, HD, T), BF16),
        v((NH, 2, T, HD), BF16),
        v((NH, 2, T, HD), BF16),
        v((NH, 2, T, HD), BF16),
        v((NH, 2, T, HD), BF16),
        v((NH, T, HD), BF16),
        v((NH, T, HD), BF16),
        v((NH, T, HD), BF16),
        v((NH, T, HD), BF16),
        v((4, NH * RANK, T), BF16),
        v((3, NH * RANK, T), BF16),
        v((NH, RANK, T), F32),
        v((RANK, T), BF16),
        v((7, RANK, T), BF16),
        v((16, 8, W), F32),
        v((16, 8, W), F32),
        v((2, 4, 8, W), F32),
        v((4, 4, 2, 16, W), BF16),
        v((4, 16, W), BF16),
        pltpu.SemaphoreType.DMA((NSEM,)),
        pltpu.SemaphoreType.DMA((NSEM,)),
        pltpu.SemaphoreType.DMA((16,)),
    ]


def per_device(query, key, value, cotangent, slots, counts, guidance, weight, lowering, raising):
    hbm = pl.BlockSpec(memory_space=pl.ANY)
    smem = pl.BlockSpec(memory_space=pltpu.SMEM)
    vmem = pl.BlockSpec(memory_space=pltpu.VMEM)
    shapes = (
        jax.ShapeDtypeStruct((T, W), BF16),
        jax.ShapeDtypeStruct((T, W), BF16),
        jax.ShapeDtypeStruct((T, W), BF16),
        jax.ShapeDtypeStruct((RANK, W), F32),
        jax.ShapeDtypeStruct((RANK, 8 * W), F32),
    )
    parts = pl.pallas_call(
        kernel,
        out_shape=shapes,
        in_specs=[hbm] * 7 + [smem] * 3,
        out_specs=(vmem,) * 5,
        scratch_shapes=scratch(),
        compiler_params=pltpu.CompilerParams(
            collective_id=0, has_side_effects=True, vmem_limit_bytes=56 * 2 ** 20
        ),
        cost_estimate=pl.CostEstimate(flops=10**10, bytes_accessed=8 * 10**6, transcendentals=3 * 10**6),
    )(query[0], key[0], value[0], cotangent, weight, lowering.T, raising, slots, counts, guidance)
    dq, dk, dv, slope, gup = pl.pallas_call(
        hand_over,
        out_shape=shapes,
        in_specs=[vmem] * 5,
        out_specs=(vmem,) * 5,
        cost_estimate=pl.CostEstimate(flops=0, bytes_accessed=4 * 10**6, transcendentals=0),
    )(*parts)
    return dq[None], dk[None], dv[None], slope.T, gup


def solution(mesh):
    in_specs = (
        P("cfg", "seq", "head"),
        P("cfg", "seq", "head"),
        P("cfg", "seq", "head"),
        P("seq", ("head", "cfg")),
        P("seq", None),
        P("seq"),
        P(),
        P("head", None),
        P("head", None),
        P(),
    )
    out_specs = (
        P("cfg", "seq", "head"),
        P("cfg", "seq", "head"),
        P("cfg", "seq", "head"),
        P("head", None),
        P(),
    )
    return jax.shard_map(
        per_device, mesh=mesh, in_specs=in_specs, out_specs=out_specs, check_vma=False
    )
```

```python
import functools
import math

import jax
import jax.numpy as jnp
from jax import lax
from jax.experimental import pallas as pl
from jax.experimental.pallas import tpu as pltpu
from jax.sharding import PartitionSpec as P

HD = 128
NH = 3
W = 384
T = 256
NK = 1024
RANK = 64
SCALE = HD ** -0.5
C2 = SCALE * math.log2(math.e)
BIG = 3.0e38
F32 = jnp.float32
BF16 = jnp.bfloat16
MESH = pl.DeviceIdType.MESH
NSEM = 128


def nn(a, b):
    return lax.dot_general(a, b, (((1,), (0,)), ((), ())), preferred_element_type=F32)


def nt(a, b):
    return lax.dot_general(a, b, (((1,), (1,)), ((), ())), preferred_element_type=F32)


def tn(a, b):
    return lax.dot_general(a, b, (((0,), (0,)), ((), ())), preferred_element_type=F32)


def kernel(
    q_in, k_in, v_in, cot_in, w_in, low_in, up_in, slots_ref, counts_ref, guide_ref,
    dq_out, dk_out, dv_out, slope_out, gup_out,
    Q, K, V, KT, VT, COT, WB, LOW, PART, PARTR, DOT, BIAS, PR, OT, STO, STR, DLO, DLR,
    DK, DV, DQ, DQB, DQR, DKB, DVB, DKR, DVR, DKX, DVX, DKXR, DVXR,
    LHB, LHR, LHO, LHY, LHYR, GSB, GSR, S1, GU, SL,
    send_sem, recv_sem, loc_sem,
):
    s, hy, c = lax.axis_index("seq"), lax.axis_index("head"), lax.axis_index("cfg")
    z, x, kc = s // 4, (s // 2) % 2, s % 2
    g = s % 4
    px = [x, x, 1 - x, 1 - x]
    pk = [kc, 1 - kc, kc, 1 - kc]
    peer = {"cfg": {"cfg": 1 - c}}
    for r in range(4):
        for d in range(4):
            if (r == 0) != (d == 0):
                peer["s%d%d" % (d, r)] = {"seq": ((z + d) % 4) * 4 + px[r] * 2 + pk[r]}
        if r:
            peer["c%d" % r] = {"seq": z * 4 + px[r] * 2 + pk[r], "cfg": 1 - c}
    for d in (1, 2, 3):
        peer["y%d" % d] = {"head": (hy + d) % 4}
        for t in (1, 2, 3):
            peer["yz%d%d" % (d, t)] = {"head": (hy + d) % 4, "seq": ((z + t) % 4) * 4 + g}
    for name, alias in (("sib", "s01"), ("x", "s02"), ("xo", "s03"), ("z1", "s10"), ("z2", "s20"), ("z3", "s30")):
        peer[name] = peer[alias]
    everyone = [name for name in peer if name not in ("sib", "x", "xo", "z1", "z2", "z3")]

    count = [0, 0]
    started = []

    def local(src, dst):
        cp = pltpu.make_async_copy(src, dst, loc_sem.at[count[1]])
        count[1] += 1
        cp.start()
        return cp

    def send(src, dst, to):
        i = count[0]
        count[0] += 1
        cp = pltpu.make_async_remote_copy(
            src_ref=src, dst_ref=dst, send_sem=send_sem.at[i], recv_sem=recv_sem.at[i],
            device_id=peer[to], device_id_type=MESH,
        )
        cp.start()
        started.append(cp)
        return cp

    def ring(axis, src, dst):
        got = {}
        for d in (1, 3, 2):
            e = (4 - d) % 4
            got[e] = send(src(d), dst(e), "%s%d" % (axis, d))
        return got

    l_cot = local(cot_in, COT.at[0])
    l_w = []
    for j in range(4):
        col = pl.multiple_of((((hy + j) % 4) * 2 + c) * W, 128)
        l_w.append(local(w_in.at[:, pl.ds(col, W)], WB.at[j, pl.ds(RANK, W)]))
        l_w.append(local(up_in.at[:, pl.ds(col, W)], WB.at[j, pl.ds(0, RANK)]))
    l_kv = [local(k_in, K.at[pl.ds(0, T)]), local(v_in, V.at[pl.ds(0, T)])]
    l_q = local(q_in, Q.at[pl.ds(0, T)])
    l_low = local(low_in, LOW)

    barrier = pltpu.get_barrier_semaphore()
    for name in everyone:
        pl.semaphore_signal(barrier, inc=1, device_id=peer[name], device_id_type=MESH)
    pl.semaphore_wait(barrier, len(everyone))

    r_cot = {4 - d: send(cot_in, COT.at[4 - d], "y%d" % d) for d in (1, 3)}
    r_k = {}
    r_v = {}
    for to, r in (("sib", 1), ("x", 2)):
        r_k[r] = send(k_in, K.at[pl.ds(r * T, T)], to)
        r_v[r] = send(v_in, V.at[pl.ds(r * T, T)], to)
    r_q = {4 - d: send(q_in, Q.at[pl.ds((4 - d) * T, T)], "z%d" % d) for d in (1, 3)}

    row = lax.broadcasted_iota(jnp.int32, (8, T), 0)
    lane = lax.broadcasted_iota(jnp.int32, (8, T), 1)
    rx, rk = row // 4, (row // 2) % 2
    gx = x + rx - 2 * x * rx
    gk = kc + rk - 2 * kc * rk
    base_block = 2 * (gx * 2 + gk) + row % 2
    for d in range(4):
        block = base_block + 8 * ((z + d) % 4)
        live = jnp.zeros((8, T), F32)
        for qb in range(2):
            n = counts_ref[qb]
            for j in range(16):
                want = jnp.where(j < n, slots_ref[qb, j], -1)
                hit = jnp.logical_and(block == want, lane // 128 == qb)
                live = jnp.where(hit, 1.0, live)
        BIAS[d] = jnp.where(live > 0, BIG, -BIG)
    r_bias = ring("z", lambda d: BIAS.at[d], lambda e: BIAS.at[4 + e])

    weight = 1.5 + 0.5 * guide_ref[0].astype(F32)
    coef = jnp.where(c == 0, weight, 1.0 - weight)

    first = {}

    def forward(d, half):
        ks = slice(half * NK // 2, (half + 1) * NK // 2)
        bias = BIAS[4 + d] if d else BIAS[0]
        bias = bias[half * 4:half * 4 + 4]
        for h in range(NH):
            hs = slice(h * HD, (h + 1) * HD)
            sc = nt(K[ks, hs], Q[d * T:(d + 1) * T, hs])
            sc = jnp.minimum(sc.reshape(4, 128, T), bias[:, None, :]).reshape(NK // 2, T)
            top = jnp.max(sc, axis=0, keepdims=True) * C2
            p = jnp.exp2(sc * C2 - top)
            total = jnp.sum(p, axis=0, keepdims=True)
            pb = p.astype(BF16)
            PR[h, ks, d * T:(d + 1) * T] = pb
            o = nn(VT[h, :, ks], pb)
            if half == 0:
                OT[h, d] = o
                first[h, d] = (top, total)
            else:
                top0, total0 = first[h, d]
                m = jnp.maximum(top, top0)
                a0, a1 = jnp.exp2(top0 - m), jnp.exp2(top - m)
                total = total0 * a0 + total * a1
                inv = 1.0 / total
                OT[h, d] = OT[h, d] * (a0 * inv) + o * (a1 * inv)
                STO[4 * h + d:4 * h + d + 1] = m + jnp.log2(total)
                tops[h, d] = (top0, top)
                low = nn(LOW[:, hs], OT[h, d].astype(BF16))
                if d:
                    LHB[d, h * RANK:(h + 1) * RANK] = low.astype(BF16)
                else:
                    LHO[h] = low
        if half and d:
            r_lh[(4 - d) % 4] = send(LHB.at[d], LHR.at[3 - d], "z%d" % d)

    tops, r_lh = {}, {}
    for cp in l_kv:
        cp.wait()
    l_q.wait()
    r_k[1].wait_recv()
    r_v[1].wait_recv()
    for h in range(NH):
        VT[h, :, :NK // 2] = V[:NK // 2, h * HD:(h + 1) * HD].T
    forward(0, 0)
    for d in (1, 3):
        r_cot[d].wait_recv()
    head, tail = pl.ds(0, T // 2), pl.ds(T // 2, T // 2)
    far_cot = [
        send(COT.at[3, head], COT.at[2, head], "y1"),
        send(COT.at[1, tail], COT.at[2, tail], "y3"),
    ]
    for d in (1, 3):
        r_q[d].wait_recv()
    far_q = [
        send(Q.at[pl.ds(3 * T, T // 2)], Q.at[pl.ds(2 * T, T // 2)], "z1"),
        send(Q.at[pl.ds(T + T // 2, T // 2)], Q.at[pl.ds(2 * T + T // 2, T // 2)], "z3"),
    ]
    l_cot.wait()
    for cp in l_w:
        cp.wait()
    bands = [slice(0, RANK + HD), slice(RANK + HD, RANK + 2 * HD), slice(RANK + 2 * HD, RANK + 3 * HD)]
    accs = [nt(WB[0, b], COT[0]) + nt(WB[1, b], COT[1]) + nt(WB[3, b], COT[3]) for b in bands]
    for d in (1, 3):
        r_bias[d].wait_recv()
        forward(d, 0)

    r_k[2].wait_recv()
    r_k[3] = send(K.at[pl.ds(2 * T, T)], K.at[pl.ds(3 * T, T)], "sib")
    r_v[2].wait_recv()
    r_v[3] = send(V.at[pl.ds(2 * T, T)], V.at[pl.ds(3 * T, T)], "sib")
    for cp in far_cot:
        cp.wait_recv()
    r_part = []
    for band, acc in zip(bands, accs):
        PART[band] = (acc + nt(WB[2, band], COT[2])).astype(BF16)
        r_part.append(send(PART.at[band], PARTR.at[band], "cfg"))

    for cp in far_q:
        cp.wait_recv()
    r_bias[2].wait_recv()
    forward(2, 0)
    r_k[3].wait_recv()
    r_v[3].wait_recv()
    for h in range(NH):
        VT[h, :, NK // 2:] = V[NK // 2:, h * HD:(h + 1) * HD].T

    l_low.wait()
    r_do = []

    def send_do(h):
        band = bands[h]
        r_part[h].wait_recv()
        base = (PART[band].astype(F32) + PARTR[band].astype(F32)) * coef
        if h == 0:
            DOT[0, :RANK] = base[:RANK].astype(BF16)
            base = base[RANK:]
        hs = slice(h * HD, (h + 1) * HD)
        DOT[0, RANK + h * HD:RANK + (h + 1) * HD] = (base + tn(LOW[:, hs], DOT[0, :RANK])).astype(BF16)
        r_do.append({4 - d: send(DOT.at[0, band], DOT.at[4 - d, band], "z%d" % d) for d in (1, 3)})

    def relay_do(h):
        lo, n = bands[h].start, bands[h].stop - bands[h].start
        one = pl.ds(lo, n // 2)
        two = pl.ds(lo + n // 2, n // 2)
        r_do[h][3].wait_recv()
        a = send(DOT.at[3, one], DOT.at[2, one], "z1")
        r_do[h][1].wait_recv()
        b = send(DOT.at[1, two], DOT.at[2, two], "z3")
        r_do[h][2] = [a, b]

    forward(2, 1)
    forward(1, 1)
    send_do(0)
    forward(3, 1)
    send_do(1)
    forward(0, 1)
    STO[4 * NH:] = jnp.zeros((16 - 4 * NH, T), F32)
    r_st = ring("z", lambda d: STO, lambda e: STR.at[e - 1])
    relay_do(0)
    send_do(2)
    for h in range(NH):
        KT[h] = K[:, h * HD:(h + 1) * HD].T

    r_dl = []

    def send_delta(h):
        for d in (0, 1, 3, 2):
            if d == 2:
                for cp in r_do[h][2]:
                    cp.wait_recv()
            do = DOT[d, RANK + h * HD:RANK + (h + 1) * HD].astype(F32)
            DLO[h, d:d + 1] = jnp.sum(do * OT[h, d], axis=0, keepdims=True)
        DLO[h, 4:] = jnp.zeros((4, T), F32)
        r_dl.append(ring("z", lambda d: DLO.at[h], lambda e: DLR.at[h, e - 1]))

    send_delta(0)
    relay_do(1)
    for e in (1, 3, 2):
        r_st[e].wait_recv()
    fac, share = {}, {}
    for d in (0, 1, 3, 2):
        for h in range(NH):
            parts = [STO[4 * h + d:4 * h + d + 1]]
            for e in (1, 2, 3):
                i = 4 * h + (d - e) % 4
                parts.append(STR[e - 1, i:i + 1])
            top = functools.reduce(jnp.maximum, parts)
            ws = [jnp.exp2(p - top) for p in parts]
            inv = 1.0 / (ws[0] + ws[1] + ws[2] + ws[3])
            share[h, d] = [w * inv for w in ws]
            fac[h, d] = [jnp.exp2(m - top) * inv for m in tops[h, d]]
        if d == 0:
            lhz = functools.reduce(lambda a, b: a + b, [LHO[h] * share[h, 0][0] for h in range(NH)])
            for e in (1, 3, 2):
                r_lh[e].wait_recv()
                for h in range(NH):
                    lhz += LHR[e - 1, h * RANK:(h + 1) * RANK].astype(F32) * share[h, 0][e]
            lhz = lhz * coef
            LHY[...] = lhz.astype(BF16)
            r_lhy = send(LHY, LHYR, "cfg")
    relay_do(2)
    send_delta(1)
    slope = [jnp.zeros((RANK, HD), F32) for _ in range(NH)]
    for d in (0, 1, 3, 2):
        for h in range(NH):
            slope[h] += nt(DOT[d, :RANK], (OT[h, d] * share[h, d][0]).astype(BF16))

    delta = {}

    def get_delta(h):
        for e in (1, 3, 2):
            r_dl[h][e].wait_recv()
        for d in range(4):
            dels = [DLO[h, d:d + 1]] + [DLR[h, e - 1, (d - e) % 4:(d - e) % 4 + 1] for e in (1, 2, 3)]
            delta[h, d] = functools.reduce(lambda a, b: a + b, [w * v for w, v in zip(share[h, d], dels)])

    r_dq, r_dks, r_dvs, r_dkx, r_dvx = {}, {}, {}, {}, {}

    def back(h, half, d):
        hs = slice(h * HD, (h + 1) * HD)
        ks = slice(half * NK // 2, (half + 1) * NK // 2)
        qs = slice(d * T, (d + 1) * T)
        do = DOT[d, RANK + h * HD:RANK + (h + 1) * HD]
        dp = nn(V[ks, hs], do)
        p = PR[h, ks, qs].astype(F32) * fac[h, d][half]
        ds = (p * (dp - delta[h, d])).astype(BF16)
        dk = nn(ds, Q[qs, hs])
        dv = nt(p.astype(BF16), do)
        dq = nn(KT[h, :, ks], ds) * SCALE
        if half == 1:
            DQ[h, d] = dq
        else:
            dq += DQ[h, d]
            if d == 0:
                DQ[h, 0] = dq
            else:
                DQB[h, d] = dq.astype(BF16)
                r_dq[h, (4 - d) % 4] = send(DQB.at[h, d], DQR.at[h, 3 - d], "z%d" % d)
        return dk, dv

    def half_done(h, half, dk, dv):
        ks = slice(half * NK // 2, (half + 1) * NK // 2)
        dk = dk * SCALE
        DK[h, ks] = dk
        DV[h, ks] = dv
        r = 1 + 2 * half
        DKB[h, half] = dk[T:].astype(BF16)
        DVB[h, half] = dv[T:].astype(BF16)
        r_dks[h, r] = send(DKB.at[h, half], DKR.at[h, 1 - half], "sib")
        r_dvs[h, r] = send(DVB.at[h, half], DVR.at[h, 1 - half], "sib")

    def cross(h):
        rows = slice(2 * T, 3 * T)
        r_dks[h, 3].wait_recv()
        DKX[h] = (DK[h, rows] + DKR[h, 0].astype(F32)).astype(BF16)
        r_dkx[h] = send(DKX.at[h], DKXR.at[h], "x")
        r_dvs[h, 3].wait_recv()
        DVX[h] = (DV[h, rows] + DVR[h, 0].astype(F32)).astype(BF16)
        r_dvx[h] = send(DVX.at[h], DVXR.at[h], "x")

    def finish(h):
        hs = slice(h * HD, (h + 1) * HD)
        dq = DQ[h, 0]
        for e in (1, 3, 2):
            r_dq[h, e].wait_recv()
            dq += DQR[h, e - 1].astype(F32)
        dq_out[:, hs] = dq.T.astype(BF16)
        for out, own, near, far, r_near, r_far in (
            (dk_out, DK, DKR, DKXR, r_dks, r_dkx),
            (dv_out, DV, DVR, DVXR, r_dvs, r_dvx),
        ):
            r_near[h, 1].wait_recv()
            r_far[h].wait_recv()
            out[:, hs] = (own[h, 0:T] + near[h, 1].astype(F32) + far[h].astype(F32)).astype(BF16)

    chain = {}

    def chain_gup():
        r_lhy.wait_recv()
        lhs = (lhz + LHYR[...].astype(F32)).astype(BF16)
        for j in range(4):
            gup = nn(lhs, COT[j]).astype(BF16)
            for t in range(4):
                GSB[t, j, 0:16] = gup[t * 16:(t + 1) * 16]
        for h in range(NH):
            for t in range(4):
                GSB[t, 0, 16:32, h * HD:(h + 1) * HD] = slope[h][t * 16:(t + 1) * 16].astype(BF16)
        chain["gs"] = []
        for t in (1, 3, 2, 0):
            for d in (1, 3, 2, 0):
                if t or d:
                    to = "yz%d%d" % (d, t) if t and d else "z%d" % t if t else "y%d" % d
                    rows = pl.ds(0, 16 if d else 32)
                    src = GSB.at[(z + t) % 4, d, rows]
                    chain["gs"].append(send(src, GSR.at[(4 - t) % 4, (4 - d) % 4, rows], to))

    def chain_plane():
        for cp in chain["gs"]:
            cp.wait_recv()
        gu = GSB[z, 0, 0:16].astype(F32)
        sl = GSB[z, 0, 16:32].astype(F32)
        for t in range(4):
            for d in range(4):
                if t or d:
                    gu += GSR[t, d, 0:16].astype(F32)
            if t:
                sl += GSR[t, 0, 16:32].astype(F32)
        S1[c, g, 0:16] = gu.astype(BF16)
        S1[c, g, 16:32] = sl.astype(BF16)
        names = ("sib", "x", "xo", "cfg", "c1", "c2", "c3")
        chain["s1"] = [send(S1.at[c, g], S1.at[c, g], to) for to in names]

    def chain_yz():
        for cp in chain["s1"]:
            cp.wait_recv()
        both = []
        for b in range(2):
            both.append(S1[b, 0].astype(F32) + S1[b, 1].astype(F32) + S1[b, 2].astype(F32) + S1[b, 3].astype(F32))
            GU[0, 0, b] = both[b][0:16].astype(BF16)
        SL[0] = (both[0][16:32] + both[1][16:32]).astype(BF16)
        chain["sl"] = ring("z", lambda d: SL.at[0], lambda e: SL.at[e])
        chain["gu"] = ring("y", lambda d: GU.at[0, 0], lambda e: GU.at[0, e])
        chain["guz"] = ring("z", lambda d: GU.at[0, 0], lambda e: GU.at[e, 0])
        for d in (1, 3, 2):
            for t in (1, 3, 2):
                cp = send(GU.at[0, 0], GU.at[4 - t, 4 - d], "yz%d%d" % (d, t))
                chain["gu"][4 * d + t] = cp

    def chain_end():
        for cp in chain["gu"].values():
            cp.wait_recv()
        for e in (1, 3, 2):
            chain["guz"][e].wait_recv()
            chain["sl"][e].wait_recv()
        for d in range(4):
            rows = pl.ds(pl.multiple_of(((z + d) % 4) * 16, 16), 16)
            slope_out[rows] = SL[d].astype(F32)
            for j in range(4):
                for b in range(2):
                    col = pl.multiple_of((((hy + j) % 4) * 2 + b) * W, 128)
                    gup_out[rows, pl.ds(col, W)] = GU[d, j, b].astype(F32)

    chain_gup()
    get_delta(0)
    hooks = {
        (0, 1, 1): [lambda: send_delta(2)],
        (0, 0, 1): [lambda: cross(0)],
        (0, 0, 3): [lambda: get_delta(1)],
        (1, 1, 3): [chain_plane],
        (1, 0, 1): [lambda: cross(1)],
        (1, 0, 3): [lambda: get_delta(2)],
        (2, 0, 0): [chain_yz],
        (2, 0, 1): [lambda: cross(2)],
    }
    for h in range(NH):
        for half in (1, 0):
            dk, dv = None, None
            for step, d in enumerate((1, 3, 2, 0)):
                a, b = back(h, half, d)
                dk = a if dk is None else dk + a
                dv = b if dv is None else dv + b
                if step == 3:
                    half_done(h, half, dk, dv)
                for hook in hooks.get((h, half, step), []):
                    hook()
    finish(0)
    finish(1)
    finish(2)
    chain_end()
    for cp in started:
        cp.wait_send()


def hand_over(*refs):
    n = len(refs) // 3
    sems = refs[-1]
    reads = [pltpu.make_async_copy(refs[i], refs[2 * n + i], sems.at[i]) for i in range(n)]
    writes = [pltpu.make_async_copy(refs[2 * n + i], refs[n + i], sems.at[n + i]) for i in range(n)]
    order = (4, 0, 1, 2, 3)
    for i in order:
        reads[i].start()
    for i in order:
        reads[i].wait()
        writes[i].start()
    for i in order:
        writes[i].wait()


def scratch():
    v = pltpu.VMEM
    return [
        v((4 * T, W), BF16),
        v((NK, W), BF16),
        v((NK, W), BF16),
        v((NH, HD, NK), BF16),
        v((NH, HD, NK), BF16),
        v((4, T, W), BF16),
        v((4, W + RANK, W), BF16),
        v((RANK, W), BF16),
        v((W + RANK, T), BF16),
        v((W + RANK, T), BF16),
        v((4, W + RANK, T), BF16),
        v((8, 8, T), F32),
        v((NH, NK, 4 * T), BF16),
        v((NH, 4, HD, T), F32),
        v((16, T), F32),
        v((3, 16, T), F32),
        v((NH, 8, T), F32),
        v((NH, 3, 8, T), F32),
        v((NH, NK, HD), F32),
        v((NH, NK, HD), F32),
        v((NH, 4, HD, T), F32),
        v((NH, 4, HD, T), BF16),
        v((NH, 3, HD, T), BF16),
        v((NH, 2, T, HD), BF16),
        v((NH, 2, T, HD), BF16),
        v((NH, 2, T, HD), BF16),
        v((NH, 2, T, HD), BF16),
        v((NH, T, HD), BF16),
        v((NH, T, HD), BF16),
        v((NH, T, HD), BF16),
        v((NH, T, HD), BF16),
        v((4, NH * RANK, T), BF16),
        v((3, NH * RANK, T), BF16),
        v((NH, RANK, T), F32),
        v((RANK, T), BF16),
        v((RANK, T), BF16),
        v((4, 4, 32, W), BF16),
        v((4, 4, 32, W), BF16),
        v((2, 4, 32, W), BF16),
        v((4, 4, 2, 16, W), BF16),
        v((4, 16, W), BF16),
        pltpu.SemaphoreType.DMA((NSEM,)),
        pltpu.SemaphoreType.DMA((NSEM,)),
        pltpu.SemaphoreType.DMA((16,)),
    ]


def per_device(query, key, value, cotangent, slots, counts, guidance, weight, lowering, raising):
    hbm = pl.BlockSpec(memory_space=pl.ANY)
    smem = pl.BlockSpec(memory_space=pltpu.SMEM)
    vmem = pl.BlockSpec(memory_space=pltpu.VMEM)
    shapes = (
        jax.ShapeDtypeStruct((T, W), BF16),
        jax.ShapeDtypeStruct((T, W), BF16),
        jax.ShapeDtypeStruct((T, W), BF16),
        jax.ShapeDtypeStruct((RANK, W), F32),
        jax.ShapeDtypeStruct((RANK, 8 * W), F32),
    )
    parts = pl.pallas_call(
        kernel,
        out_shape=shapes,
        in_specs=[hbm] * 7 + [smem] * 3,
        out_specs=(vmem,) * 5,
        scratch_shapes=scratch(),
        compiler_params=pltpu.CompilerParams(
            collective_id=0, has_side_effects=True, vmem_limit_bytes=56 * 2 ** 20
        ),
        cost_estimate=pl.CostEstimate(flops=10**10, bytes_accessed=8 * 10**6, transcendentals=3 * 10**6),
    )(query[0], key[0], value[0], cotangent, weight, lowering.T, raising, slots, counts, guidance)
    dq, dk, dv, slope, gup = pl.pallas_call(
        hand_over,
        out_shape=shapes,
        in_specs=[hbm] * 5,
        out_specs=(hbm,) * 5,
        scratch_shapes=[pltpu.VMEM(a.shape, a.dtype) for a in shapes] + [pltpu.SemaphoreType.DMA((10,))],
        cost_estimate=pl.CostEstimate(flops=0, bytes_accessed=4 * 10**6, transcendentals=0),
    )(*parts)
    return dq[None], dk[None], dv[None], slope.T, gup


def solution(mesh):
    in_specs = (
        P("cfg", "seq", "head"),
        P("cfg", "seq", "head"),
        P("cfg", "seq", "head"),
        P("seq", ("head", "cfg")),
        P("seq", None),
        P("seq"),
        P(),
        P("head", None),
        P("head", None),
        P(),
    )
    out_specs = (
        P("cfg", "seq", "head"),
        P("cfg", "seq", "head"),
        P("cfg", "seq", "head"),
        P("head", None),
        P(),
    )
    return jax.shard_map(
        per_device, mesh=mesh, in_specs=in_specs, out_specs=out_specs, check_vma=False
    )
```

```python
import functools
import math

import jax
import jax.numpy as jnp
from jax import lax
from jax.experimental import pallas as pl
from jax.experimental.pallas import tpu as pltpu
from jax.sharding import PartitionSpec as P

HD = 128
NH = 3
W = 384
T = 256
NK = 1024
RANK = 64
SCALE = HD ** -0.5
C2 = SCALE * math.log2(math.e)
BIG = 3.0e38
F32 = jnp.float32
BF16 = jnp.bfloat16
MESH = pl.DeviceIdType.MESH
NSEM = 128


def nn(a, b):
    return lax.dot_general(a, b, (((1,), (0,)), ((), ())), preferred_element_type=F32)


def nt(a, b):
    return lax.dot_general(a, b, (((1,), (1,)), ((), ())), preferred_element_type=F32)


def tn(a, b):
    return lax.dot_general(a, b, (((0,), (0,)), ((), ())), preferred_element_type=F32)


def kernel(
    q_in, k_in, v_in, cot_in, w_in, low_in, up_in, slots_ref, counts_ref, guide_ref,
    dq_out, dk_out, dv_out, slope_out, gup_out,
    Q, K, V, KT, VT, COT, WB, LOW, PART, PARTR, DOT, BIAS, PR, OT, STO, STR, DLO, DLR,
    DK, DV, DQ, DQB, DQR, DKB, DVB, DKR, DVR, DKX, DVX, DKXR, DVXR,
    LHB, LHR, LHO, LHY, LHYR, GSB, GSR, S1, GU, SL,
    send_sem, recv_sem, loc_sem,
):
    s, hy, c = lax.axis_index("seq"), lax.axis_index("head"), lax.axis_index("cfg")
    z, x, kc = s // 4, (s // 2) % 2, s % 2
    g = s % 4
    px = [x, x, 1 - x, 1 - x]
    pk = [kc, 1 - kc, kc, 1 - kc]
    peer = {"cfg": {"cfg": 1 - c}}
    for r in range(4):
        for d in range(4):
            if (r == 0) != (d == 0):
                peer["s%d%d" % (d, r)] = {"seq": ((z + d) % 4) * 4 + px[r] * 2 + pk[r]}
        if r:
            peer["c%d" % r] = {"seq": z * 4 + px[r] * 2 + pk[r], "cfg": 1 - c}
    for d in (1, 2, 3):
        peer["y%d" % d] = {"head": (hy + d) % 4}
        for t in (1, 2, 3):
            peer["yz%d%d" % (d, t)] = {"head": (hy + d) % 4, "seq": ((z + t) % 4) * 4 + g}
    for name, alias in (("sib", "s01"), ("x", "s02"), ("xo", "s03"), ("z1", "s10"), ("z2", "s20"), ("z3", "s30")):
        peer[name] = peer[alias]
    everyone = [name for name in peer if name not in ("sib", "x", "xo", "z1", "z2", "z3")]

    count = [0, 0]
    started = []

    def local(src, dst):
        cp = pltpu.make_async_copy(src, dst, loc_sem.at[count[1]])
        count[1] += 1
        cp.start()
        return cp

    def send(src, dst, to):
        i = count[0]
        count[0] += 1
        cp = pltpu.make_async_remote_copy(
            src_ref=src, dst_ref=dst, send_sem=send_sem.at[i], recv_sem=recv_sem.at[i],
            device_id=peer[to], device_id_type=MESH,
        )
        cp.start()
        started.append(cp)
        return cp

    def ring(axis, src, dst):
        got = {}
        for d in (1, 3, 2):
            e = (4 - d) % 4
            got[e] = send(src(d), dst(e), "%s%d" % (axis, d))
        return got

    l_cot = local(cot_in, COT.at[0])
    l_w = []
    for j in range(4):
        col = pl.multiple_of((((hy + j) % 4) * 2 + c) * W, 128)
        l_w.append(local(w_in.at[:, pl.ds(col, W)], WB.at[j, pl.ds(RANK, W)]))
        l_w.append(local(up_in.at[:, pl.ds(col, W)], WB.at[j, pl.ds(0, RANK)]))
    l_kv = [local(k_in, K.at[pl.ds(0, T)]), local(v_in, V.at[pl.ds(0, T)])]
    l_q = local(q_in, Q.at[pl.ds(0, T)])
    l_low = local(low_in, LOW)

    barrier = pltpu.get_barrier_semaphore()
    for name in everyone:
        pl.semaphore_signal(barrier, inc=1, device_id=peer[name], device_id_type=MESH)
    pl.semaphore_wait(barrier, len(everyone))

    r_cot = {4 - d: send(cot_in, COT.at[4 - d], "y%d" % d) for d in (1, 3)}
    r_k = {}
    r_v = {}
    for to, r in (("sib", 1), ("x", 2)):
        r_k[r] = send(k_in, K.at[pl.ds(r * T, T)], to)
        r_v[r] = send(v_in, V.at[pl.ds(r * T, T)], to)
    r_q = {4 - d: send(q_in, Q.at[pl.ds((4 - d) * T, T)], "z%d" % d) for d in (1, 3)}

    row = lax.broadcasted_iota(jnp.int32, (8, T), 0)
    lane = lax.broadcasted_iota(jnp.int32, (8, T), 1)
    rx, rk = row // 4, (row // 2) % 2
    gx = x + rx - 2 * x * rx
    gk = kc + rk - 2 * kc * rk
    base_block = 2 * (gx * 2 + gk) + row % 2
    for d in range(4):
        block = base_block + 8 * ((z + d) % 4)
        live = jnp.zeros((8, T), F32)
        for qb in range(2):
            n = counts_ref[qb]
            for j in range(16):
                want = jnp.where(j < n, slots_ref[qb, j], -1)
                hit = jnp.logical_and(block == want, lane // 128 == qb)
                live = jnp.where(hit, 1.0, live)
        BIAS[d] = jnp.where(live > 0, BIG, -BIG)
    r_bias = ring("z", lambda d: BIAS.at[d], lambda e: BIAS.at[4 + e])

    weight = 1.5 + 0.5 * guide_ref[0].astype(F32)
    coef = jnp.where(c == 0, weight, 1.0 - weight)

    first = {}

    def forward(d, half):
        ks = slice(half * NK // 2, (half + 1) * NK // 2)
        bias = BIAS[4 + d] if d else BIAS[0]
        bias = bias[half * 4:half * 4 + 4]
        for h in range(NH):
            hs = slice(h * HD, (h + 1) * HD)
            sc = nt(K[ks, hs], Q[d * T:(d + 1) * T, hs])
            sc = jnp.minimum(sc.reshape(4, 128, T), bias[:, None, :]).reshape(NK // 2, T)
            top = jnp.max(sc, axis=0, keepdims=True) * C2
            p = jnp.exp2(sc * C2 - top)
            total = jnp.sum(p, axis=0, keepdims=True)
            pb = p.astype(BF16)
            PR[h, ks, d * T:(d + 1) * T] = pb
            o = nn(VT[h, :, ks], pb)
            if half == 0:
                OT[h, d] = o
                first[h, d] = (top, total)
            else:
                top0, total0 = first[h, d]
                m = jnp.maximum(top, top0)
                a0, a1 = jnp.exp2(top0 - m), jnp.exp2(top - m)
                total = total0 * a0 + total * a1
                inv = 1.0 / total
                OT[h, d] = OT[h, d] * (a0 * inv) + o * (a1 * inv)
                STO[4 * h + d:4 * h + d + 1] = m + jnp.log2(total)
                tops[h, d] = (top0, top)
                low = nn(LOW[:, hs], OT[h, d].astype(BF16))
                if d:
                    LHB[d, h * RANK:(h + 1) * RANK] = low.astype(BF16)
                else:
                    LHO[h] = low
        if half and d:
            r_lh[(4 - d) % 4] = send(LHB.at[d], LHR.at[3 - d], "z%d" % d)

    tops, r_lh = {}, {}
    for cp in l_kv:
        cp.wait()
    l_q.wait()
    r_k[1].wait_recv()
    r_v[1].wait_recv()
    for h in range(NH):
        VT[h, :, :NK // 2] = V[:NK // 2, h * HD:(h + 1) * HD].T
    forward(0, 0)
    for d in (1, 3):
        r_cot[d].wait_recv()
    head, tail = pl.ds(0, T // 2), pl.ds(T // 2, T // 2)
    far_cot = [
        send(COT.at[3, head], COT.at[2, head], "y1"),
        send(COT.at[1, tail], COT.at[2, tail], "y3"),
    ]
    for d in (1, 3):
        r_q[d].wait_recv()
    far_q = [
        send(Q.at[pl.ds(3 * T, T // 2)], Q.at[pl.ds(2 * T, T // 2)], "z1"),
        send(Q.at[pl.ds(T + T // 2, T // 2)], Q.at[pl.ds(2 * T + T // 2, T // 2)], "z3"),
    ]
    l_cot.wait()
    for cp in l_w:
        cp.wait()
    bands = [slice(0, RANK + HD), slice(RANK + HD, RANK + 2 * HD), slice(RANK + 2 * HD, RANK + 3 * HD)]
    accs = [nt(WB[0, b], COT[0]) + nt(WB[1, b], COT[1]) + nt(WB[3, b], COT[3]) for b in bands]
    for d in (1, 3):
        r_bias[d].wait_recv()
        forward(d, 0)

    r_k[2].wait_recv()
    r_k[3] = send(K.at[pl.ds(2 * T, T)], K.at[pl.ds(3 * T, T)], "sib")
    r_v[2].wait_recv()
    r_v[3] = send(V.at[pl.ds(2 * T, T)], V.at[pl.ds(3 * T, T)], "sib")
    for cp in far_cot:
        cp.wait_recv()
    r_part = []
    for band, acc in zip(bands, accs):
        PART[band] = (acc + nt(WB[2, band], COT[2])).astype(BF16)
        r_part.append(send(PART.at[band], PARTR.at[band], "cfg"))

    for cp in far_q:
        cp.wait_recv()
    r_bias[2].wait_recv()
    forward(2, 0)
    r_k[3].wait_recv()
    r_v[3].wait_recv()
    for h in range(NH):
        VT[h, :, NK // 2:] = V[NK // 2:, h * HD:(h + 1) * HD].T

    l_low.wait()
    r_do = []

    def send_do(h):
        band = bands[h]
        r_part[h].wait_recv()
        base = (PART[band].astype(F32) + PARTR[band].astype(F32)) * coef
        if h == 0:
            DOT[0, :RANK] = base[:RANK].astype(BF16)
            base = base[RANK:]
        hs = slice(h * HD, (h + 1) * HD)
        DOT[0, RANK + h * HD:RANK + (h + 1) * HD] = (base + tn(LOW[:, hs], DOT[0, :RANK])).astype(BF16)
        r_do.append({4 - d: send(DOT.at[0, band], DOT.at[4 - d, band], "z%d" % d) for d in (1, 3)})

    def relay_do(h):
        lo, n = bands[h].start, bands[h].stop - bands[h].start
        one = pl.ds(lo, n // 2)
        two = pl.ds(lo + n // 2, n // 2)
        r_do[h][3].wait_recv()
        a = send(DOT.at[3, one], DOT.at[2, one], "z1")
        r_do[h][1].wait_recv()
        b = send(DOT.at[1, two], DOT.at[2, two], "z3")
        r_do[h][2] = [a, b]

    forward(2, 1)
    send_do(0)
    forward(1, 1)
    send_do(1)
    forward(3, 1)
    send_do(2)
    forward(0, 1)
    STO[4 * NH:] = jnp.zeros((16 - 4 * NH, T), F32)
    r_st = ring("z", lambda d: STO, lambda e: STR.at[e - 1])
    relay_do(0)
    relay_do(1)
    for h in range(NH):
        KT[h] = K[:, h * HD:(h + 1) * HD].T

    r_dl = []

    def send_delta(h):
        for d in (0, 1, 3, 2):
            if d == 2:
                for cp in r_do[h][2]:
                    cp.wait_recv()
            do = DOT[d, RANK + h * HD:RANK + (h + 1) * HD].astype(F32)
            DLO[h, d:d + 1] = jnp.sum(do * OT[h, d], axis=0, keepdims=True)
        DLO[h, 4:] = jnp.zeros((4, T), F32)
        r_dl.append(ring("z", lambda d: DLO.at[h], lambda e: DLR.at[h, e - 1]))

    relay_do(2)
    for e in (1, 3, 2):
        r_st[e].wait_recv()
    fac, share = {}, {}
    for d in (0, 1, 3, 2):
        for h in range(NH):
            parts = [STO[4 * h + d:4 * h + d + 1]]
            for e in (1, 2, 3):
                i = 4 * h + (d - e) % 4
                parts.append(STR[e - 1, i:i + 1])
            top = functools.reduce(jnp.maximum, parts)
            ws = [jnp.exp2(p - top) for p in parts]
            inv = 1.0 / (ws[0] + ws[1] + ws[2] + ws[3])
            share[h, d] = [w * inv for w in ws]
            fac[h, d] = [jnp.exp2(m - top) * inv for m in tops[h, d]]
        if d == 0:
            lhz = functools.reduce(lambda a, b: a + b, [LHO[h] * share[h, 0][0] for h in range(NH)])
            for e in (1, 3, 2):
                r_lh[e].wait_recv()
                for h in range(NH):
                    lhz += LHR[e - 1, h * RANK:(h + 1) * RANK].astype(F32) * share[h, 0][e]
            lhz = lhz * coef
            LHY[...] = lhz.astype(BF16)
            r_lhy = send(LHY, LHYR, "cfg")
    send_delta(0)
    send_delta(1)
    send_delta(2)
    slope = [jnp.zeros((RANK, HD), F32) for _ in range(NH)]
    for d in (0, 1, 3, 2):
        for h in range(NH):
            slope[h] += nt(DOT[d, :RANK], (OT[h, d] * share[h, d][0]).astype(BF16))

    delta = {}

    def get_delta(h):
        for e in (1, 3, 2):
            r_dl[h][e].wait_recv()
        for d in range(4):
            dels = [DLO[h, d:d + 1]] + [DLR[h, e - 1, (d - e) % 4:(d - e) % 4 + 1] for e in (1, 2, 3)]
            delta[h, d] = functools.reduce(lambda a, b: a + b, [w * v for w, v in zip(share[h, d], dels)])

    r_dq, r_dks, r_dvs, r_dkx, r_dvx = {}, {}, {}, {}, {}

    def back(h, half, d):
        hs = slice(h * HD, (h + 1) * HD)
        ks = slice(half * NK // 2, (half + 1) * NK // 2)
        qs = slice(d * T, (d + 1) * T)
        do = DOT[d, RANK + h * HD:RANK + (h + 1) * HD]
        dp = nn(V[ks, hs], do)
        p = PR[h, ks, qs].astype(F32) * fac[h, d][half]
        ds = (p * (dp - delta[h, d])).astype(BF16)
        dk = nn(ds, Q[qs, hs])
        dv = nt(p.astype(BF16), do)
        dq = nn(KT[h, :, ks], ds) * SCALE
        if half == 1:
            DQ[h, d] = dq
        else:
            dq += DQ[h, d]
            if d == 0:
                DQ[h, 0] = dq
            else:
                DQB[h, d] = dq.astype(BF16)
                r_dq[h, (4 - d) % 4] = send(DQB.at[h, d], DQR.at[h, 3 - d], "z%d" % d)
        return dk, dv

    def half_done(h, half, dk, dv):
        ks = slice(half * NK // 2, (half + 1) * NK // 2)
        dk = dk * SCALE
        DK[h, ks] = dk
        DV[h, ks] = dv
        r = 1 + 2 * half
        DKB[h, half] = dk[T:].astype(BF16)
        DVB[h, half] = dv[T:].astype(BF16)
        r_dks[h, r] = send(DKB.at[h, half], DKR.at[h, 1 - half], "sib")
        r_dvs[h, r] = send(DVB.at[h, half], DVR.at[h, 1 - half], "sib")

    def cross(h):
        rows = slice(2 * T, 3 * T)
        r_dks[h, 3].wait_recv()
        DKX[h] = (DK[h, rows] + DKR[h, 0].astype(F32)).astype(BF16)
        r_dkx[h] = send(DKX.at[h], DKXR.at[h], "x")
        r_dvs[h, 3].wait_recv()
        DVX[h] = (DV[h, rows] + DVR[h, 0].astype(F32)).astype(BF16)
        r_dvx[h] = send(DVX.at[h], DVXR.at[h], "x")

    def finish(h):
        hs = slice(h * HD, (h + 1) * HD)
        dq = DQ[h, 0]
        for e in (1, 3, 2):
            r_dq[h, e].wait_recv()
            dq += DQR[h, e - 1].astype(F32)
        dq_out[:, hs] = dq.T.astype(BF16)
        for out, own, near, far, r_near, r_far in (
            (dk_out, DK, DKR, DKXR, r_dks, r_dkx),
            (dv_out, DV, DVR, DVXR, r_dvs, r_dvx),
        ):
            r_near[h, 1].wait_recv()
            r_far[h].wait_recv()
            out[:, hs] = (own[h, 0:T] + near[h, 1].astype(F32) + far[h].astype(F32)).astype(BF16)

    chain = {}

    def chain_gup():
        r_lhy.wait_recv()
        lhs = (lhz + LHYR[...].astype(F32)).astype(BF16)
        for j in range(4):
            gup = nn(lhs, COT[j]).astype(BF16)
            for t in range(4):
                GSB[t, j, 0:16] = gup[t * 16:(t + 1) * 16]
        for h in range(NH):
            for t in range(4):
                GSB[t, 0, 16:32, h * HD:(h + 1) * HD] = slope[h][t * 16:(t + 1) * 16].astype(BF16)
        chain["gs"] = []
        for t in (1, 3, 2, 0):
            for d in (1, 3, 2, 0):
                if t or d:
                    to = "yz%d%d" % (d, t) if t and d else "z%d" % t if t else "y%d" % d
                    rows = pl.ds(0, 16 if d else 32)
                    src = GSB.at[(z + t) % 4, d, rows]
                    chain["gs"].append(send(src, GSR.at[(4 - t) % 4, (4 - d) % 4, rows], to))

    def chain_plane():
        for cp in chain["gs"]:
            cp.wait_recv()
        gu = GSB[z, 0, 0:16].astype(F32)
        sl = GSB[z, 0, 16:32].astype(F32)
        for t in range(4):
            for d in range(4):
                if t or d:
                    gu += GSR[t, d, 0:16].astype(F32)
            if t:
                sl += GSR[t, 0, 16:32].astype(F32)
        S1[c, g, 0:16] = gu.astype(BF16)
        S1[c, g, 16:32] = sl.astype(BF16)
        names = ("sib", "x", "xo", "cfg", "c1", "c2", "c3")
        chain["s1"] = [send(S1.at[c, g], S1.at[c, g], to) for to in names]

    def chain_yz():
        for cp in chain["s1"]:
            cp.wait_recv()
        both = []
        for b in range(2):
            both.append(S1[b, 0].astype(F32) + S1[b, 1].astype(F32) + S1[b, 2].astype(F32) + S1[b, 3].astype(F32))
            GU[0, 0, b] = both[b][0:16].astype(BF16)
        SL[0] = (both[0][16:32] + both[1][16:32]).astype(BF16)
        chain["sl"] = ring("z", lambda d: SL.at[0], lambda e: SL.at[e])
        chain["gu"] = ring("y", lambda d: GU.at[0, 0], lambda e: GU.at[0, e])
        chain["guz"] = ring("z", lambda d: GU.at[0, 0], lambda e: GU.at[e, 0])
        for d in (1, 3, 2):
            for t in (1, 3, 2):
                cp = send(GU.at[0, 0], GU.at[4 - t, 4 - d], "yz%d%d" % (d, t))
                chain["gu"][4 * d + t] = cp

    def chain_end():
        for cp in chain["gu"].values():
            cp.wait_recv()
        for e in (1, 3, 2):
            chain["guz"][e].wait_recv()
            chain["sl"][e].wait_recv()
        for d in range(4):
            rows = pl.ds(pl.multiple_of(((z + d) % 4) * 16, 16), 16)
            slope_out[rows] = SL[d].astype(F32)
            for j in range(4):
                for b in range(2):
                    col = pl.multiple_of((((hy + j) % 4) * 2 + b) * W, 128)
                    gup_out[rows, pl.ds(col, W)] = GU[d, j, b].astype(F32)

    chain_gup()
    get_delta(0)
    hooks = {
        (0, 0, 1): [lambda: cross(0)],
        (0, 0, 3): [lambda: get_delta(1)],
        (1, 1, 3): [chain_plane],
        (1, 0, 1): [lambda: cross(1)],
        (1, 0, 3): [lambda: get_delta(2)],
        (2, 0, 0): [chain_yz],
        (2, 0, 1): [lambda: cross(2)],
    }
    for h in range(NH):
        for half in (1, 0):
            dk, dv = None, None
            for step, d in enumerate((1, 3, 2, 0)):
                a, b = back(h, half, d)
                dk = a if dk is None else dk + a
                dv = b if dv is None else dv + b
                if step == 3:
                    half_done(h, half, dk, dv)
                for hook in hooks.get((h, half, step), []):
                    hook()
    finish(0)
    finish(1)
    finish(2)
    chain_end()
    for cp in started:
        cp.wait_send()


def hand_over(*refs):
    n = len(refs) // 3
    sems = refs[-1]
    reads = [pltpu.make_async_copy(refs[i], refs[2 * n + i], sems.at[i]) for i in range(n)]
    writes = [pltpu.make_async_copy(refs[2 * n + i], refs[n + i], sems.at[n + i]) for i in range(n)]
    order = (4, 0, 1, 2, 3)
    for i in order:
        reads[i].start()
    for i in order:
        reads[i].wait()
        writes[i].start()
    for i in order:
        writes[i].wait()


def scratch():
    v = pltpu.VMEM
    return [
        v((4 * T, W), BF16),
        v((NK, W), BF16),
        v((NK, W), BF16),
        v((NH, HD, NK), BF16),
        v((NH, HD, NK), BF16),
        v((4, T, W), BF16),
        v((4, W + RANK, W), BF16),
        v((RANK, W), BF16),
        v((W + RANK, T), BF16),
        v((W + RANK, T), BF16),
        v((4, W + RANK, T), BF16),
        v((8, 8, T), F32),
        v((NH, NK, 4 * T), BF16),
        v((NH, 4, HD, T), F32),
        v((16, T), F32),
        v((3, 16, T), F32),
        v((NH, 8, T), F32),
        v((NH, 3, 8, T), F32),
        v((NH, NK, HD), F32),
        v((NH, NK, HD), F32),
        v((NH, 4, HD, T), F32),
        v((NH, 4, HD, T), BF16),
        v((NH, 3, HD, T), BF16),
        v((NH, 2, T, HD), BF16),
        v((NH, 2, T, HD), BF16),
        v((NH, 2, T, HD), BF16),
        v((NH, 2, T, HD), BF16),
        v((NH, T, HD), BF16),
        v((NH, T, HD), BF16),
        v((NH, T, HD), BF16),
        v((NH, T, HD), BF16),
        v((4, NH * RANK, T), BF16),
        v((3, NH * RANK, T), BF16),
        v((NH, RANK, T), F32),
        v((RANK, T), BF16),
        v((RANK, T), BF16),
        v((4, 4, 32, W), BF16),
        v((4, 4, 32, W), BF16),
        v((2, 4, 32, W), BF16),
        v((4, 4, 2, 16, W), BF16),
        v((4, 16, W), BF16),
        pltpu.SemaphoreType.DMA((NSEM,)),
        pltpu.SemaphoreType.DMA((NSEM,)),
        pltpu.SemaphoreType.DMA((16,)),
    ]


def per_device(query, key, value, cotangent, slots, counts, guidance, weight, lowering, raising):
    hbm = pl.BlockSpec(memory_space=pl.ANY)
    smem = pl.BlockSpec(memory_space=pltpu.SMEM)
    vmem = pl.BlockSpec(memory_space=pltpu.VMEM)
    shapes = (
        jax.ShapeDtypeStruct((T, W), BF16),
        jax.ShapeDtypeStruct((T, W), BF16),
        jax.ShapeDtypeStruct((T, W), BF16),
        jax.ShapeDtypeStruct((RANK, W), F32),
        jax.ShapeDtypeStruct((RANK, 8 * W), F32),
    )
    parts = pl.pallas_call(
        kernel,
        out_shape=shapes,
        in_specs=[hbm] * 7 + [smem] * 3,
        out_specs=(vmem,) * 5,
        scratch_shapes=scratch(),
        compiler_params=pltpu.CompilerParams(
            collective_id=0, has_side_effects=True, vmem_limit_bytes=56 * 2 ** 20
        ),
        cost_estimate=pl.CostEstimate(flops=10**10, bytes_accessed=8 * 10**6, transcendentals=3 * 10**6),
    )(query[0], key[0], value[0], cotangent, weight, lowering.T, raising, slots, counts, guidance)
    dq, dk, dv, slope, gup = pl.pallas_call(
        hand_over,
        out_shape=shapes,
        in_specs=[hbm] * 5,
        out_specs=(hbm,) * 5,
        scratch_shapes=[pltpu.VMEM(a.shape, a.dtype) for a in shapes] + [pltpu.SemaphoreType.DMA((10,))],
        cost_estimate=pl.CostEstimate(flops=0, bytes_accessed=4 * 10**6, transcendentals=0),
    )(*parts)
    return dq[None], dk[None], dv[None], slope.T, gup


def solution(mesh):
    in_specs = (
        P("cfg", "seq", "head"),
        P("cfg", "seq", "head"),
        P("cfg", "seq", "head"),
        P("seq", ("head", "cfg")),
        P("seq", None),
        P("seq"),
        P(),
        P("head", None),
        P("head", None),
        P(),
    )
    out_specs = (
        P("cfg", "seq", "head"),
        P("cfg", "seq", "head"),
        P("cfg", "seq", "head"),
        P("head", None),
        P(),
    )
    return jax.shard_map(
        per_device, mesh=mesh, in_specs=in_specs, out_specs=out_specs, check_vma=False
    )
```
